32 devices in a mesh: wide: 16 (over z, y, core), narrow: 2 (over x).
Axes of the slice: x: 2, y: 2, z: 4, core: 2. Of those that a mesh axis runs over, the one named last changes fastest.
Arguments:
- images: bfloat16 [2048, 72, 256], P('wide'), may hold values from -512 to 512
- defocus: float32 [2048], P('wide'), may hold values from 1 to 3
- class_index: int32 [2048], P('wide'), may hold values from 0 to 47
- rotation_index: int32 [2048], P('wide'), may hold values from 0 to 71
- owner_map: int32 [48], replicated, may hold values from 0 to 15, as said below
- roster: int32 [2, 3], replicated, may hold values from 0 to 15, as said below
- ref_store: bfloat16 [16, 2, 8, 72, 256], P('wide', 'narrow'), may hold values from -0.25 to 0.25
Outputs:
- new_references: bfloat16 [16, 2, 4, 72, 256], P('wide', 'narrow')
- log_evidence: float32 [2048], P('wide')
The draws below stay inside these ranges and needn't reach their ends.
Inputs may be any that keep to these rules, and one draw needn't show every extreme that they name: Each row of roster names 3 different indices. `owner_map`: in each group of 24 consecutive classes, no index is named more than 4 times, and one index is named exactly 4 times.
All inputs are finite; a program needn't handle non-finite values.
Results may differ from the reference program's by a relative error of at most 0.0038.
The reference program's roundings to bfloat16 on the way (of `references`, `weighted` and `aligned`) count: a program that leaves them out, or rounds other values in their place, can miss the bound.
Values may be sent and summed in bfloat16 or wider, within the bound.
A program may use at most 128 MiB of HBM per device.

```python
import math
import jax
import jax.numpy as jnp
from jax import lax

CYCLES = 128
ANGLES = 72
BLOCK = 8
STEPS = 3
OWN_MAX = 4
CLS_GRP = 24
CLASSES = 48
SIGMA_ROT = 8
PART = 2048
N_WIDE = 16
N_NARROW = 2


def ref_values(key):
    base_key, scale_key = jax.random.split(jax.random.fold_in(key, 7))
    shape_all = (N_WIDE, N_NARROW, BLOCK, ANGLES, 2 * CYCLES)
    scales = jnp.exp(jax.random.uniform(scale_key, (N_WIDE, N_NARROW, BLOCK, 1, 1), jnp.float32, math.log(0.01), math.log(0.04)))
    values = jnp.clip(jax.random.normal(base_key, shape_all, jnp.float32), -6.0, 6.0)
    return (values * scales).astype(jnp.bfloat16)


def draw_ref_store(key, part):
    return ref_values(key)


def defocus_values(key):
    spread = jax.random.uniform(jax.random.fold_in(key, 31), (PART,), jnp.float32, 0.0, math.log(3.0))
    return jnp.exp(spread)


def draw_defocus(key, part):
    return defocus_values(key)


def class_values(key):
    return jax.random.randint(jax.random.fold_in(key, 37), (PART,), 0, CLASSES).astype(jnp.int32)


def draw_class_index(key, part):
    return class_values(key)


def rotation_values(key):
    return jax.random.randint(jax.random.fold_in(key, 41), (PART,), 0, ANGLES).astype(jnp.int32)


def draw_rotation_index(key, part):
    return rotation_values(key)


def owners_of_group(group_key):
    rank_key, pool_key = jax.random.split(group_key)
    ranking = jax.random.permutation(rank_key, CLS_GRP).astype(jnp.int32)
    pool = jax.random.permutation(pool_key, N_WIDE).astype(jnp.int32)
    position = jnp.where(ranking < OWN_MAX, 0, 1 + (ranking - OWN_MAX) // 2)
    return pool[position]


def draw_owner_map(key, part):
    group_keys = jax.random.split(jax.random.fold_in(key, 11), N_NARROW)
    return jax.vmap(owners_of_group)(group_keys).reshape(CLASSES).astype(jnp.int32)


def holders_of_group(group_key):
    return jax.random.permutation(group_key, N_WIDE)[:STEPS].astype(jnp.int32)


def roster_values(key):
    group_keys = jax.random.split(jax.random.fold_in(key, 23), N_NARROW)
    return jax.vmap(holders_of_group)(group_keys).astype(jnp.int32)


def draw_roster(key, part):
    return roster_values(key)


def contrast_of(defocus_rows):
    cycle_freq = (jnp.arange(CYCLES, dtype=jnp.float32) + 1.0) / CYCLES
    phase_angle = 8.0 * math.pi * defocus_rows[:, None] * cycle_freq[None, :] ** 2
    return -jnp.sin(phase_angle) - 0.1 * jnp.cos(phase_angle)


def draw_images(key, part):
    base_key = jax.random.fold_in(jax.random.fold_in(key, 5), 0)
    values = jnp.clip(jax.random.normal(base_key, (PART, ANGLES, 2 * CYCLES), jnp.float32), -6.0, 6.0)
    planted_count = PART // 64
    rows = jnp.arange(planted_count, dtype=jnp.int32) * 64 + 5
    refs = ref_values(key).astype(jnp.float32)
    roster = roster_values(key)
    chosen = class_values(key)[rows]
    centre = rotation_values(key)[rows]
    group_ids = chosen // CLS_GRP
    step_ids = chosen % CLS_GRP // BLOCK
    slot_ids = chosen % BLOCK
    holders = roster[group_ids, step_ids]
    picked = refs[holders, group_ids, slot_ids]
    contrast_rows = contrast_of(defocus_values(key)[rows])
    squares = jnp.sum(picked * picked, axis=1)
    power = ANGLES * (squares[:, :CYCLES] + squares[:, CYCLES:])
    energy = jnp.sum(contrast_rows * contrast_rows * power, axis=-1)
    ranks = jax.random.permutation(jax.random.fold_in(key, 43), planted_count).astype(jnp.float32)
    target = 110.0 + 140.0 * ranks / max(planted_count - 1, 1)
    sigma = float(SIGMA_ROT)
    first_amp = 0.5 + target * ANGLES / energy
    second_amp = 0.5 + (target - 2.0 + 0.5 / (sigma * sigma)) * ANGLES / energy
    counting = jnp.arange(ANGLES, dtype=jnp.int32)
    first_src = (counting[None, :] - centre[:, None]) % ANGLES
    second_src = (counting[None, :] - centre[:, None] - 1) % ANGLES
    first_turn = jnp.take_along_axis(picked, first_src[:, :, None], axis=1)
    second_turn = jnp.take_along_axis(picked, second_src[:, :, None], axis=1)
    doubled = jnp.concatenate([contrast_rows, contrast_rows], axis=-1)
    planted = (first_amp[:, None, None] * first_turn + second_amp[:, None, None] * second_turn) * doubled[:, None, :]
    values = values.at[rows].add(planted)
    return jnp.clip(values, -512.0, 512.0).astype(jnp.bfloat16)


def setup_inputs(seed: int = 0) -> dict:
    keys = jax.random.split(jax.random.key(seed), 8)
    images = draw_images(jax.random.fold_in(keys[7], 71), 0)
    defocus = draw_defocus(jax.random.fold_in(keys[7], 71), 0)
    class_index = draw_class_index(jax.random.fold_in(keys[7], 71), 0)
    rotation_index = draw_rotation_index(jax.random.fold_in(keys[7], 71), 0)
    owner_map = draw_owner_map(jax.random.fold_in(keys[7], 71), 0)
    roster = draw_roster(jax.random.fold_in(keys[7], 71), 0)
    ref_store = draw_ref_store(jax.random.fold_in(keys[7], 71), 0)
    return {"images": images, "defocus": defocus, "class_index": class_index, "rotation_index": rotation_index, "owner_map": owner_map, "roster": roster, "ref_store": ref_store}


TAU = 1.0
CONTRAST = 0.1
TOP_PRECISION = lax.Precision.HIGHEST


def angle_tables(length):
    counting = jnp.arange(length, dtype=jnp.int32)
    products = (counting[:, None] * counting[None, :]) % length
    phase_angle = products.astype(jnp.float32) * (2.0 * math.pi / length)
    return jnp.cos(phase_angle), jnp.sin(phase_angle)


def contrast(defocus_rows):
    cycle_freq = (jnp.arange(CYCLES, dtype=jnp.float32) + 1.0) / CYCLES
    phase_angle = 8.0 * math.pi * defocus_rows[:, None] * cycle_freq[None, :] ** 2
    return -jnp.sin(phase_angle) - CONTRAST * jnp.cos(phase_angle)


def spectrum(polar, cosines_low, sines_low):
    polar_wide = polar.astype(jnp.float32)
    cos_part = jnp.einsum("ma,naj->nmj", cosines_low.astype(jnp.float32), polar_wide)
    sin_part = jnp.einsum("ma,naj->nmj", sines_low.astype(jnp.float32), polar_wide)
    real_part = cos_part[..., :CYCLES] + sin_part[..., CYCLES:]
    imag_part = cos_part[..., CYCLES:] - sin_part[..., :CYCLES]
    return jnp.concatenate([real_part, imag_part], axis=-1).astype(jnp.bfloat16)


def rotation_prior(rotation_rows):
    counting = jnp.arange(ANGLES, dtype=jnp.int32)
    distance = jnp.abs(counting[None, :] - rotation_rows[:, None])
    distance = jnp.minimum(distance, ANGLES - distance).astype(jnp.float32)
    return -0.5 * (distance / SIGMA_ROT) ** 2


def polar_image(harmonic, cosine_table, sine_table):
    real_part = harmonic[..., :CYCLES]
    imag_part = harmonic[..., CYCLES:]
    polar_real = (jnp.einsum("cmk,ma->cak", real_part, cosine_table, precision=TOP_PRECISION) - jnp.einsum("cmk,ma->cak", imag_part, sine_table, precision=TOP_PRECISION)) / ANGLES
    polar_imag = (jnp.einsum("cmk,ma->cak", imag_part, cosine_table, precision=TOP_PRECISION) + jnp.einsum("cmk,ma->cak", real_part, sine_table, precision=TOP_PRECISION)) / ANGLES
    return jnp.concatenate([polar_real, polar_imag], axis=-1)


def reference(images, defocus, class_index, rotation_index, owner_map, roster, ref_store):
    cosine_table, sine_table = angle_tables(ANGLES)
    cosines_low = cosine_table.astype(jnp.bfloat16)
    sines_low = sine_table.astype(jnp.bfloat16)
    class_ids = jnp.arange(CLASSES, dtype=jnp.int32)
    group_ids = class_ids // CLS_GRP
    step_ids = (class_ids % CLS_GRP) // BLOCK
    slot_numbers = class_ids % BLOCK
    holders = roster[group_ids, step_ids]
    references = ref_store[holders, group_ids, slot_numbers]
    ref_spec = spectrum(references, cosines_low, sines_low)
    ref_swap = jnp.concatenate([-ref_spec[..., CYCLES:], ref_spec[..., :CYCLES]], axis=-1)
    ref_wide = ref_spec.astype(jnp.float32)
    swap_wide = ref_swap.astype(jnp.float32)
    power = jnp.sum(jnp.square(ref_wide), axis=1)
    power = power[:, :CYCLES] + power[:, CYCLES:]
    rows_block = math.gcd(PART, 256)
    blocks_count = PART // rows_block
    feature_len = ANGLES * 2 * CYCLES

    def scan_block(carried, inputs):
        numerator, denominator = carried
        image_rows, defocus_rows, class_rows, rotation_rows = inputs
        contrast_rows = contrast(defocus_rows)
        doubled = jnp.concatenate([contrast_rows, contrast_rows], axis=-1)
        weighted = (image_rows.astype(jnp.float32) * doubled[:, None, :]).astype(jnp.bfloat16)
        spectra = spectrum(weighted, cosines_low, sines_low)
        spectra_wide = spectra.astype(jnp.float32)
        real_correlation = jnp.einsum("pmj,cmj->pcm", spectra_wide, ref_wide)
        imaginary_correlation = jnp.einsum("pmj,cmj->pcm", spectra_wide, swap_wide)
        turned_images = jnp.einsum("exj,ji->exi", real_correlation, cosine_table, precision=TOP_PRECISION) - jnp.einsum("exj,ji->exi", imaginary_correlation, sine_table, precision=TOP_PRECISION)
        energy = jnp.dot(contrast_rows * contrast_rows, power.T, precision=TOP_PRECISION)
        scores = (turned_images - 0.5 * energy[:, :, None]) / ANGLES + rotation_prior(rotation_rows)[:, None, :]
        running_max = jnp.max(scores, axis=(1, 2))
        evidence = running_max + jnp.log(jnp.sum(jnp.exp(scores - running_max[:, None, None]), axis=(1, 2)))
        own_scores = jnp.take_along_axis(scores, class_rows[:, None, None].astype(jnp.int32), axis=1)[:, 0, :]
        weight = jax.nn.softmax(own_scores, axis=-1)
        h_real = jnp.dot(weight, cosine_table, precision=TOP_PRECISION)
        h_imag = jnp.dot(weight, sine_table, precision=TOP_PRECISION)
        x_real = spectra_wide[..., :CYCLES]
        x_imag = spectra_wide[..., CYCLES:]
        a_real = x_real * h_real[:, :, None] - x_imag * h_imag[:, :, None]
        a_imag = x_real * h_imag[:, :, None] + x_imag * h_real[:, :, None]
        aligned = jnp.concatenate([a_real, a_imag], axis=-1).astype(jnp.bfloat16)
        numerator = numerator + jax.ops.segment_sum(aligned.astype(jnp.float32).reshape(rows_block, feature_len), class_rows, num_segments=CLASSES)
        denominator = denominator + jax.ops.segment_sum(contrast_rows * contrast_rows, class_rows, num_segments=CLASSES)
        return (numerator, denominator), evidence

    start = (jnp.zeros((CLASSES, feature_len), jnp.float32), jnp.zeros((CLASSES, CYCLES), jnp.float32))
    inputs = (images.reshape(blocks_count, rows_block, ANGLES, 2 * CYCLES), defocus.reshape(blocks_count, rows_block), class_index.reshape(blocks_count, rows_block), rotation_index.reshape(blocks_count, rows_block))
    (numerator, denominator), evidence = lax.scan(scan_block, start, inputs)
    doubled_den = jnp.concatenate([denominator, denominator], axis=-1)
    harmonic = numerator.reshape(CLASSES, ANGLES, 2 * CYCLES) / (doubled_den[:, None, :] + TAU)
    polar = polar_image(harmonic, cosine_table, sine_table)
    owners = owner_map.reshape(N_NARROW, CLS_GRP)
    wide_ids = jnp.arange(N_WIDE, dtype=jnp.int32)
    matches = (owners[:, None, :] == wide_ids[None, :, None]).astype(jnp.int32)
    ranking = jnp.cumsum(matches, axis=2) - 1
    slot_range = jnp.arange(OWN_MAX, dtype=jnp.int32)
    slot_pick = ((matches[:, :, None, :] == 1) & (ranking[:, :, None, :] == slot_range[None, None, :, None])).astype(jnp.float32)
    grouped = polar.reshape(N_NARROW, CLS_GRP, feature_len)
    placed = jnp.einsum("gwsc,gcf->wgsf", slot_pick, grouped, precision=TOP_PRECISION)
    new_references = placed.reshape(N_WIDE, N_NARROW, OWN_MAX, ANGLES, 2 * CYCLES).astype(jnp.bfloat16)
    return new_references, evidence.reshape(PART)
```

```python
import functools
import math

import jax
import jax.numpy as jnp
from jax import lax
from jax.experimental import pallas as pl
from jax.experimental.pallas import tpu as pltpu
from jax.sharding import PartitionSpec as P

CYCLES = 128
ANGLES = 72
STEPS = 3
OWN_MAX = 4
CLS_GRP = 24
SIGMA_ROT = 8
TAU = 1.0
CONTRAST = 0.1
TOP_PRECISION = lax.Precision.HIGHEST
MESH = pl.DeviceIdType.MESH
VMEM_LIMIT = 48 * 1024 * 1024


def up(value, step):
    return -(-value // step) * step


def angle_tables(length):
    counting = jnp.arange(length, dtype=jnp.int32)
    products = counting[:, None] * counting[None, :] % length
    phase_angle = products.astype(jnp.float32) * (2.0 * math.pi / length)
    return (jnp.cos(phase_angle), jnp.sin(phase_angle))


def contrast(defocus_rows):
    cycle_freq = (jnp.arange(CYCLES, dtype=jnp.float32) + 1.0) / CYCLES
    phase_angle = 8.0 * math.pi * defocus_rows[:, None] * cycle_freq[None, :] ** 2
    return -jnp.sin(phase_angle) - CONTRAST * jnp.cos(phase_angle)


def spectrum(polar, cosines_low, sines_low):
    cos_part = jnp.einsum("ma,naj->nmj", cosines_low, polar, preferred_element_type=jnp.float32)
    sin_part = jnp.einsum("ma,naj->nmj", sines_low, polar, preferred_element_type=jnp.float32)
    real_part = cos_part[..., :CYCLES] + sin_part[..., CYCLES:]
    imag_part = cos_part[..., CYCLES:] - sin_part[..., :CYCLES]
    return jnp.concatenate([real_part, imag_part], axis=-1).astype(jnp.bfloat16)


def rotation_prior(rotation_rows):
    counting = jnp.arange(ANGLES, dtype=jnp.int32)
    distance = jnp.abs(counting[None, :] - rotation_rows[:, None])
    distance = jnp.minimum(distance, ANGLES - distance).astype(jnp.float32)
    return -0.5 * (distance / SIGMA_ROT) ** 2


def polar_image(harmonic, cosine_table, sine_table):
    real_part = harmonic[..., :CYCLES]
    imag_part = harmonic[..., CYCLES:]
    polar_real = (
        jnp.einsum("cmk,ma->cak", real_part, cosine_table, precision=TOP_PRECISION)
        - jnp.einsum("cmk,ma->cak", imag_part, sine_table, precision=TOP_PRECISION)
    ) / ANGLES
    polar_imag = (
        jnp.einsum("cmk,ma->cak", imag_part, cosine_table, precision=TOP_PRECISION)
        + jnp.einsum("cmk,ma->cak", real_part, sine_table, precision=TOP_PRECISION)
    ) / ANGLES
    return jnp.concatenate([polar_real, polar_imag], axis=-1)


def remote(src, dst, send_sem, recv_sem, **target):
    return pltpu.make_async_remote_copy(
        src_ref=src,
        dst_ref=dst,
        send_sem=send_sem,
        recv_sem=recv_sem,
        device_id=target,
        device_id_type=MESH,
    )


def fetch_kernel(
    wide, roster_ref, piece_ref, gath_ref, got, a_send, a_recv, b_send, b_recv, c_send, c_recv
):
    me = lax.axis_index("wide")
    chips = wide // 2
    chip, core = me // 2, lax.rem(me, 2)
    sibling = chip * 2 + 1 - core
    barrier = pltpu.get_barrier_semaphore()
    for d in range(1, wide):
        pl.semaphore_signal(
            barrier, inc=1, device_id={"wide": lax.rem(me + d, wide)}, device_id_type=MESH
        )
    pl.semaphore_wait(barrier, wide - 1)
    first = []
    for d in range(1, wide):
        peer = lax.rem(me + d, wide)
        copy = remote(piece_ref.at[peer], got.at[me], a_send.at[d], a_recv.at[d], wide=peer)
        copy.start()
        first.append(copy)
    got[me] = piece_ref[me]
    for copy in first:
        copy.wait_recv()
    for step in range(STEPS):
        gath_ref[me, step] = got[roster_ref[step]]
    second = []
    for e in range(1, chips):
        peer = lax.rem(chip + e, chips) * 2 + core
        copy = remote(gath_ref.at[me], gath_ref.at[me], b_send.at[e], b_recv.at[e], wide=peer)
        copy.start()
        second.append(copy)
    third = []
    for e in range(chips):
        origin = lax.rem(chip + chips - e, chips) * 2 + core
        if e:
            second[e - 1].wait_recv()
        copy = remote(
            gath_ref.at[origin], gath_ref.at[origin], c_send.at[e], c_recv.at[e], wide=sibling
        )
        copy.start()
        third.append(copy)
    for copy in third:
        copy.wait_recv()
    for copy in first + second + third:
        copy.wait_send()


def fetch(block, roster_row, wide):
    block_classes = block.shape[0]
    parts = max(wide // (2 * block_classes), 1)
    rows = ANGLES // parts
    padded = up(rows, 16)
    pieces = block.reshape(block_classes, parts, rows, 2, CYCLES).transpose(0, 3, 1, 2, 4)
    pieces = pieces.reshape(wide, rows, CYCLES)
    pieces = jnp.pad(pieces, ((0, 0), (0, padded - rows), (0, 0)))
    chips = wide // 2
    got = pl.pallas_call(
        functools.partial(fetch_kernel, wide),
        out_shape=jax.ShapeDtypeStruct((wide, STEPS, padded, CYCLES), jnp.bfloat16),
        in_specs=[
            pl.BlockSpec(memory_space=pltpu.SMEM),
            pl.BlockSpec(memory_space=pltpu.VMEM),
        ],
        out_specs=pl.BlockSpec(memory_space=pltpu.VMEM),
        scratch_shapes=[
            pltpu.VMEM((wide, padded, CYCLES), jnp.bfloat16),
            pltpu.SemaphoreType.DMA((wide,)),
            pltpu.SemaphoreType.DMA((wide,)),
            pltpu.SemaphoreType.DMA((chips,)),
            pltpu.SemaphoreType.DMA((chips,)),
            pltpu.SemaphoreType.DMA((chips,)),
            pltpu.SemaphoreType.DMA((chips,)),
        ],
        compiler_params=pltpu.CompilerParams(
            collective_id=0, has_side_effects=True, vmem_limit_bytes=VMEM_LIMIT
        ),
        name="fetch",
    )(roster_row, pieces)
    got = got[:, :, :rows].reshape(block_classes, 2, parts, STEPS, rows, CYCLES)
    return got.transpose(3, 0, 2, 4, 1, 5).reshape(STEPS * block_classes, ANGLES, 2 * CYCLES)


def sum_kernel(
    wide, narrow, chunk,
    num_ref, den_ref, top_ref, pick_ref, har_ref, ev_ref,
    num_got, den_got, den_all, top_got, part_out, part_got, own, slot_out,
    t_send, t_recv, d_send, d_recv, e_send, e_recv, n_send, n_recv, p_send, p_recv, s_send, s_recv,
):
    me = lax.axis_index("wide")
    col = lax.axis_index("narrow")
    chips = wide // 2
    chip, core = me // 2, lax.rem(me, 2)
    sibling = chip * 2 + 1 - core
    mine = pl.ds(pl.multiple_of(core * CYCLES, CYCLES), CYCLES)
    theirs = pl.ds(pl.multiple_of((1 - core) * CYCLES, CYCLES), CYCLES)
    barrier = pltpu.get_barrier_semaphore()
    for d in range(1, wide):
        pl.semaphore_signal(
            barrier, inc=1, device_id={"wide": lax.rem(me + d, wide)}, device_id_type=MESH
        )
    for d in range(1, narrow):
        pl.semaphore_signal(
            barrier, inc=1, device_id={"narrow": lax.rem(col + d, narrow)}, device_id_type=MESH
        )
    pl.semaphore_wait(barrier, wide + narrow - 2)
    sent = []
    den_copy = remote(den_ref, den_got, d_send.at[0], d_recv.at[0], wide=sibling)
    den_copy.start()
    sent.append(den_copy)
    halves = []
    for e in range(chips):
        place = lax.rem(chip + 1 + e, chips)
        rows = pl.ds(place * chunk, chunk)
        copy = remote(
            num_ref.at[rows, :, theirs], num_got.at[rows], n_send.at[e], n_recv.at[e], wide=sibling
        )
        copy.start()
        halves.append(copy)
    tops = []
    for d in range(1, narrow):
        copy = remote(
            top_ref, top_got.at[d], t_send.at[d], t_recv.at[d], narrow=lax.rem(col + d, narrow)
        )
        copy.start()
        tops.append(copy)
    den_copy.wait_recv()
    den_all[0] = den_ref[...] + den_got[...]
    dens = []
    for e in range(1, chips):
        peer = lax.rem(chip + e, chips) * 2 + core
        copy = remote(den_all.at[0], den_all.at[e], e_send.at[e], e_recv.at[e], wide=peer)
        copy.start()
        dens.append(copy)
    flat = chunk * CLS_GRP
    padded = up(flat, 16)
    parts = []
    for e in range(chips):
        place = lax.rem(chip + 1 + e, chips)
        rows = pl.ds(place * chunk, chunk)
        halves[e].wait_recv()
        both = num_ref[rows, :, mine] + num_got[rows]
        if e == chips - 1:
            own[...] = both
            continue
        both = both.reshape(flat, CYCLES)
        if padded > flat:
            both = jnp.concatenate([both, jnp.zeros((padded - flat, CYCLES), jnp.float32)], axis=0)
        part_out[e] = both.astype(jnp.bfloat16)
        copy = remote(
            part_out.at[e], part_got.at[e], p_send.at[e], p_recv.at[e], wide=place * 2 + core
        )
        copy.start()
        parts.append(copy)
    top = top_ref[0:1]
    total = top_ref[1:2]
    for d in range(1, narrow):
        tops[d - 1].wait_recv()
        other = top_got[d, 0:1]
        joined = jnp.maximum(top, other)
        total = total * jnp.exp(top - joined) + top_got[d, 1:2] * jnp.exp(other - joined)
        top = joined
    ev_ref[...] = jnp.broadcast_to(top + jnp.log(total), ev_ref.shape)
    for copy in dens:
        copy.wait_recv()
    scale = den_all[0]
    for e in range(1, chips):
        scale = scale + den_all[e]
    scale = 1.0 / (scale + TAU)
    for copy in parts:
        copy.wait_recv()
    summed = own[...].reshape(flat, CYCLES)
    for e in range(chips - 1):
        summed = summed + part_got[e].astype(jnp.float32)[:flat]
    summed = summed.reshape(chunk, CLS_GRP, CYCLES) * scale[None]
    pick = pick_ref[...]
    for row in range(chunk):
        chosen = jnp.dot(
            pick, summed[row], preferred_element_type=jnp.float32, precision=TOP_PRECISION
        )
        slot_out[:, row] = chosen.reshape(wide, 8, CYCLES)
    slots = []
    for d in range(1, wide):
        peer = lax.rem(me + d, wide)
        copy = remote(slot_out.at[peer], har_ref.at[me], s_send.at[d], s_recv.at[d], wide=peer)
        copy.start()
        slots.append(copy)
    har_ref[me] = slot_out[me]
    for copy in slots:
        copy.wait_recv()
    for copy in sent + halves + tops + dens + parts + slots:
        copy.wait_send()


def class_sums(numer, denom, top, total, pick, wide, narrow):
    chips = wide // 2
    chunk = -(-ANGLES // chips)
    numer = jnp.pad(numer, ((0, chunk * chips - ANGLES), (0, 0), (0, 0)))
    particles = top.shape[0]
    tops = jnp.concatenate([top[None], total[None], jnp.zeros((6, particles), jnp.float32)], axis=0)
    padded = up(chunk * CLS_GRP, 16)
    vmem = pl.BlockSpec(memory_space=pltpu.VMEM)
    dma = pltpu.SemaphoreType.DMA
    got, evidence = pl.pallas_call(
        functools.partial(sum_kernel, wide, narrow, chunk),
        out_shape=(
            jax.ShapeDtypeStruct((wide, chunk, 8, CYCLES), jnp.float32),
            jax.ShapeDtypeStruct((8, particles), jnp.float32),
        ),
        in_specs=[vmem] * 4,
        out_specs=(vmem, vmem),
        scratch_shapes=[
            pltpu.VMEM((chunk * chips, CLS_GRP, CYCLES), jnp.float32),
            pltpu.VMEM((CLS_GRP, CYCLES), jnp.float32),
            pltpu.VMEM((chips, CLS_GRP, CYCLES), jnp.float32),
            pltpu.VMEM((narrow, 8, particles), jnp.float32),
            pltpu.VMEM((chips, padded, CYCLES), jnp.bfloat16),
            pltpu.VMEM((chips, padded, CYCLES), jnp.bfloat16),
            pltpu.VMEM((chunk, CLS_GRP, CYCLES), jnp.float32),
            pltpu.VMEM((wide, chunk, 8, CYCLES), jnp.float32),
            dma((narrow,)), dma((narrow,)),
            dma((1,)), dma((1,)),
            dma((chips,)), dma((chips,)),
            dma((chips,)), dma((chips,)),
            dma((chips,)), dma((chips,)),
            dma((wide,)), dma((wide,)),
        ],
        compiler_params=pltpu.CompilerParams(
            collective_id=1, has_side_effects=True, vmem_limit_bytes=VMEM_LIMIT
        ),
        name="class_sums",
    )(numer, denom, tops, pick)
    got = got[:, :, :OWN_MAX].reshape(chips, 2, chunk, OWN_MAX, CYCLES)
    got = got.transpose(3, 0, 2, 1, 4).reshape(OWN_MAX, chips * chunk, 2 * CYCLES)
    return got[:, :ANGLES], evidence[0]


def per_device(images, defocus, class_index, rotation_index, owner_map, roster, ref_store):
    class_group = lax.axis_index("narrow")
    wide_count = lax.axis_size("wide")
    narrow_count = lax.axis_size("narrow")
    cosine_table, sine_table = angle_tables(ANGLES)
    cosines_low = cosine_table.astype(jnp.bfloat16)
    sines_low = sine_table.astype(jnp.bfloat16)
    owner_plan = lax.dynamic_index_in_dim(roster, class_group, 0, keepdims=False)
    leading_class = class_group * CLS_GRP
    refs = fetch(ref_store[0, 0], owner_plan, wide_count)
    contrast_rows = contrast(defocus)
    contrast_sq = contrast_rows * contrast_rows
    doubled = jnp.concatenate([contrast_rows, contrast_rows], axis=-1)
    weighted = (images.astype(jnp.float32) * doubled[:, None, :]).astype(jnp.bfloat16)
    spectra = spectrum(weighted, cosines_low, sines_low)
    prior_rows = rotation_prior(rotation_index)
    ref_spec = spectrum(refs, cosines_low, sines_low)
    ref_swap = jnp.concatenate([-ref_spec[..., CYCLES:], ref_spec[..., :CYCLES]], axis=-1)
    real_correlation = jnp.einsum(
        "pmj,cmj->pcm", spectra, ref_spec, preferred_element_type=jnp.float32
    )
    imaginary_correlation = jnp.einsum(
        "pmj,cmj->pcm", spectra, ref_swap, preferred_element_type=jnp.float32
    )
    turned_images = jnp.einsum(
        "exj,ji->exi", real_correlation, cosine_table, precision=TOP_PRECISION
    ) - jnp.einsum("exj,ji->exi", imaginary_correlation, sine_table, precision=TOP_PRECISION)
    power = jnp.sum(jnp.square(ref_spec.astype(jnp.float32)), axis=1)
    power = power[:, :CYCLES] + power[:, CYCLES:]
    energy = jnp.dot(contrast_sq, power.T, precision=TOP_PRECISION)
    scores = (turned_images - 0.5 * energy[:, :, None]) / ANGLES + prior_rows[:, None, :]
    class_ids = leading_class + jnp.arange(CLS_GRP, dtype=jnp.int32)
    members = class_index[None, :] == class_ids[:, None]
    matches = members.T.astype(jnp.float32)
    own_scores = jnp.einsum("pj,pjr->pr", matches, scores, precision=TOP_PRECISION)
    top = jnp.max(scores, axis=(1, 2))
    total = jnp.sum(jnp.exp(scores - top[:, None, None]), axis=(1, 2))
    weight = jax.nn.softmax(own_scores, axis=-1)
    h_real = jnp.dot(weight, cosine_table, precision=TOP_PRECISION)
    h_imag = jnp.dot(weight, sine_table, precision=TOP_PRECISION)
    spectra_wide = spectra.astype(jnp.float32)
    x_real = spectra_wide[..., :CYCLES]
    x_imag = spectra_wide[..., CYCLES:]
    a_real = x_real * h_real[:, :, None] - x_imag * h_imag[:, :, None]
    a_imag = x_real * h_imag[:, :, None] + x_imag * h_real[:, :, None]
    aligned = jnp.concatenate([a_real, a_imag], axis=-1).astype(jnp.bfloat16)
    numer_part = jnp.einsum(
        "cp,pmj->mcj", members.astype(jnp.bfloat16), aligned, preferred_element_type=jnp.float32
    )
    denom_part = jnp.dot(members.astype(jnp.float32), contrast_sq, precision=TOP_PRECISION)
    owners = lax.dynamic_slice_in_dim(owner_map, leading_class, CLS_GRP)
    held = (owners[None, :] == jnp.arange(wide_count, dtype=jnp.int32)[:, None]).astype(jnp.int32)
    ranking = jnp.cumsum(held, axis=1) - 1
    slot_range = jnp.arange(8, dtype=jnp.int32)
    slot_pick = (held[:, None, :] == 1) & (ranking[:, None, :] == slot_range[None, :, None])
    slot_pick = slot_pick.astype(jnp.float32).reshape(wide_count * 8, CLS_GRP)
    harmonic, log_evidence = class_sums(
        numer_part, denom_part, top, total, slot_pick, wide_count, narrow_count
    )
    polar = polar_image(harmonic, cosine_table, sine_table)
    new_references = polar.astype(jnp.bfloat16).reshape(1, 1, OWN_MAX, ANGLES, 2 * CYCLES)
    return (new_references, log_evidence)


def solution(mesh):
    in_specs = (
        P("wide", None, None),
        P("wide"),
        P("wide"),
        P("wide"),
        P(),
        P(),
        P("wide", "narrow", None, None, None),
    )
    out_specs = (P("wide", "narrow", None, None, None), P("wide"))
    return jax.shard_map(
        per_device, mesh=mesh, in_specs=in_specs, out_specs=out_specs, check_vma=False
    )
```

```python
import functools
import math

import jax
import jax.numpy as jnp
import numpy as np
from jax import lax
from jax.experimental import pallas as pl
from jax.experimental.pallas import tpu as pltpu
from jax.sharding import PartitionSpec as P

CYCLES = 128
ANGLES = 72
STEPS = 3
OWN_MAX = 4
CLS_GRP = 24
SIGMA_ROT = 8
TAU = 1.0
CONTRAST = 0.1
TOP = lax.Precision.HIGHEST
MESH = pl.DeviceIdType.MESH
VMEM_LIMIT = 56 * 1024 * 1024
F32 = jnp.float32
BF16 = jnp.bfloat16
TILE = 16


def up(value, step):
    return -(-value // step) * step


def tables():
    counting = np.arange(ANGLES)
    phase = (counting[:, None] * counting[None, :] % ANGLES) * (2.0 * math.pi / ANGLES)
    return np.cos(phase).astype(np.float32), np.sin(phase).astype(np.float32)


def contrast(defocus_rows):
    cycle_freq = (jnp.arange(CYCLES, dtype=F32) + 1.0) / CYCLES
    phase_angle = 8.0 * math.pi * defocus_rows[:, None] * cycle_freq[None, :] ** 2
    return -jnp.sin(phase_angle) - CONTRAST * jnp.cos(phase_angle)


def remote(src, dst, send_sem, recv_sem, **target):
    return pltpu.make_async_remote_copy(
        src_ref=src,
        dst_ref=dst,
        send_sem=send_sem,
        recv_sem=recv_sem,
        device_id=target,
        device_id_type=MESH,
    )


def exact(a, b):
    return jnp.dot(a, b, preferred_element_type=F32, precision=TOP)


def kernel(
    wide, narrow, chunk, pieces_each,
    roster_ref, piece_ref, img_hbm, con_ref, class_ref, rot_ref, owner_ref,
    dft_ref, rdft_ref, turn_ref, tab_ref, back_ref,
    new_ref, ev_ref,
    img_ref, spec, got, gath, rr, ct, sc, num, num_got, den, den_got, den_all, top, top_got,
    part_out, part_got, own, slot_out, har,
    i_sem, a_send, a_recv, b_send, b_recv, c_send, c_recv, t_send, t_recv, d_send, d_recv,
    e_send, e_recv, n_send, n_recv, p_send, p_recv, s_send, s_recv,
):
    me = lax.axis_index("wide")
    col = lax.axis_index("narrow")
    chips = wide // 2
    chip, core = me // 2, lax.rem(me, 2)
    sibling = chip * 2 + 1 - core
    particles = con_ref.shape[0]
    block_classes = CLS_GRP // STEPS
    load = pltpu.make_async_copy(img_hbm, img_ref, i_sem.at[0])
    load.start()
    barrier = pltpu.get_barrier_semaphore()
    for d in range(1, wide):
        pl.semaphore_signal(
            barrier, inc=1, device_id={"wide": lax.rem(me + d, wide)}, device_id_type=MESH
        )
    for d in range(1, narrow):
        pl.semaphore_signal(
            barrier, inc=1, device_id={"narrow": lax.rem(col + d, narrow)}, device_id_type=MESH
        )
    pl.semaphore_wait(barrier, wide + narrow - 2)

    first = []
    for d in range(1, wide):
        peer = lax.rem(me + d, wide)
        copy = remote(piece_ref.at[peer], got.at[me], a_send.at[d], a_recv.at[d], wide=peer)
        copy.start()
        first.append(copy)
    got[me] = piece_ref[me]

    class_row = lax.broadcasted_iota(jnp.int32, (CLS_GRP, particles), 0) + col * CLS_GRP
    members = (class_row == class_ref[...]).astype(F32)
    squares = jnp.square(con_ref[...])
    den[...] = exact(members, squares)
    den_copy = remote(den, den_got, d_send.at[0], d_recv.at[0], wide=sibling)
    den_copy.start()

    load.wait()
    dft = dft_ref[...]

    def spectra(group, carry):
        reals, imags = [], []
        for pair in range(TILE // 2):
            columns = []
            for which in range(2):
                row = group * TILE + pair * 2 + which
                gain = con_ref[pl.ds(row, 1), :]
                image = img_ref[row].astype(F32)
                columns.append(
                    jnp.concatenate([image[:, :CYCLES] * gain, image[:, CYCLES:] * gain], axis=0)
                )
            packed = jnp.concatenate(columns, axis=1).astype(BF16)
            out = jnp.dot(dft, packed, preferred_element_type=F32)
            for which in range(2):
                lanes = out[:, which * CYCLES : (which + 1) * CYCLES]
                reals.append(lanes[:ANGLES])
                imags.append(lanes[ANGLES:])
        rows = pl.ds(pl.multiple_of(group * TILE, TILE), TILE)
        spec[0:ANGLES, rows, 0:CYCLES] = jnp.swapaxes(jnp.stack(reals), 0, 1).astype(BF16)
        spec[0:ANGLES, rows, CYCLES:] = jnp.swapaxes(jnp.stack(imags), 0, 1).astype(BF16)
        return carry

    groups = particles // TILE
    cuts = [0, groups // 4, groups * 5 // 8, groups]
    lax.fori_loop(cuts[0], cuts[1], spectra, 0)
    if chunk * chips > ANGLES:
        spec[ANGLES:] = jnp.zeros((chunk * chips - ANGLES, particles, 2 * CYCLES), BF16)

    den_copy.wait_recv()
    den_all[0] = den[...] + den_got[...]
    dens = []
    for e in range(1, chips):
        peer = lax.rem(chip + e, chips) * 2 + core
        copy = remote(den_all.at[0], den_all.at[e], e_send.at[e], e_recv.at[e], wide=peer)
        copy.start()
        dens.append(copy)
    for copy in first:
        copy.wait_recv()
    for step in range(STEPS):
        gath[me, step] = got[roster_ref[col, step]]
    second = []
    for e in range(1, chips):
        peer = lax.rem(chip + e, chips) * 2 + core
        copy = remote(gath.at[me], gath.at[me], b_send.at[e], b_recv.at[e], wide=peer)
        copy.start()
        second.append(copy)
    lax.fori_loop(cuts[1], cuts[2], spectra, 0)
    third = []
    for e in range(chips):
        origin = lax.rem(chip + chips - e, chips) * 2 + core
        if e:
            second[e - 1].wait_recv()
        copy = remote(gath.at[origin], gath.at[origin], c_send.at[e], c_recv.at[e], wide=sibling)
        copy.start()
        third.append(copy)
    lax.fori_loop(cuts[2], cuts[3], spectra, 0)
    for copy in third:
        copy.wait_recv()

    rdft = rdft_ref[...]
    power = []
    for step in range(STEPS):
        reals, imags = [], []
        for pair in range(block_classes // 2):
            columns = []
            for slot in (2 * pair, 2 * pair + 1):
                start = slot * 2 * pieces_each
                columns.append(
                    jnp.concatenate(
                        [gath[start + k, step] for k in range(2 * pieces_each)], axis=0
                    )
                )
            out = jnp.dot(rdft, jnp.concatenate(columns, axis=1), preferred_element_type=F32)
            for which in range(2):
                lanes = out[:, which * CYCLES : (which + 1) * CYCLES]
                reals.append(lanes[:ANGLES])
                imags.append(lanes[ANGLES:])
        real = jnp.swapaxes(jnp.stack(reals), 0, 1).astype(BF16).astype(F32)
        imag = jnp.swapaxes(jnp.stack(imags), 0, 1).astype(BF16).astype(F32)
        power.append(jnp.sum(real * real + imag * imag, axis=0))
        first_rows = jnp.concatenate([real, imag], axis=-1)
        second_rows = jnp.concatenate([-imag, real], axis=-1)
        rr[:, step] = jnp.concatenate([first_rows, second_rows], axis=1).astype(BF16)
    energy = lax.dot_general(
        jnp.concatenate(power, axis=0), squares, (((1,), (1,)), ((), ())),
        preferred_element_type=F32, precision=TOP,
    )

    def correlate(m, carry):
        refs = rr[m].reshape(2 * CLS_GRP, 2 * CYCLES)
        ct[m] = lax.dot_general(
            refs, spec[m], (((1,), (1,)), ((), ())), preferred_element_type=F32
        )
        return carry

    lax.fori_loop(0, ANGLES, correlate, 0, unroll=8)

    angle = lax.broadcasted_iota(jnp.int32, (ANGLES, particles), 0)
    distance = jnp.abs(angle - rot_ref[...])
    distance = jnp.minimum(distance, ANGLES - distance).astype(F32)
    prior = -0.5 * jnp.square(distance / SIGMA_ROT)
    turn = turn_ref[...]
    chosen = jnp.zeros((ANGLES, particles), F32)
    best = None
    for step in range(STEPS):
        start = step * 2 * block_classes
        real = jnp.swapaxes(ct[:, start : start + block_classes, :], 0, 1)
        imag = jnp.swapaxes(ct[:, start + block_classes : start + 2 * block_classes, :], 0, 1)
        for pair in range(block_classes // 2):
            slots = (2 * pair, 2 * pair + 1)
            both = jnp.concatenate(
                [
                    jnp.concatenate([real[s] for s in slots], axis=1),
                    jnp.concatenate([imag[s] for s in slots], axis=1),
                ],
                axis=0,
            )
            turned = exact(turn, both)
            for which, slot in enumerate(slots):
                c = step * block_classes + slot
                lanes = turned[:, which * particles : (which + 1) * particles]
                scores = (lanes - 0.5 * energy[c : c + 1]) / ANGLES + prior
                sc[c] = scores
                chosen = chosen + members[c : c + 1] * scores
                best = scores if best is None else jnp.maximum(best, scores)
    peak = jnp.max(best, axis=0, keepdims=True)
    total = jnp.zeros((ANGLES, particles), F32)
    for c in range(CLS_GRP):
        total = total + jnp.exp(sc[c] - peak)
    top[0:1] = peak
    top[1:2] = jnp.sum(total, axis=0, keepdims=True)
    tops = []
    for d in range(1, narrow):
        copy = remote(top, top_got.at[d], t_send.at[d], t_recv.at[d], narrow=lax.rem(col + d, narrow))
        copy.start()
        tops.append(copy)
    weight = jnp.exp(chosen - jnp.max(chosen, axis=0, keepdims=True))
    weight = weight / jnp.sum(weight, axis=0, keepdims=True)
    weight = jnp.swapaxes(weight, 0, 1)
    picked = jnp.concatenate([members, jnp.zeros((8, particles), F32)], axis=0).astype(BF16)

    mine = pl.ds(pl.multiple_of(core * CYCLES, CYCLES), CYCLES)
    theirs = pl.ds(pl.multiple_of((1 - core) * CYCLES, CYCLES), CYCLES)
    flat = chunk * CLS_GRP
    padded = up(flat, 16)
    halves, parts = [], []

    def pass_on(e):
        place = lax.rem(chip + 1 + e, chips)
        rows = pl.ds(place * chunk, chunk)
        halves[e].wait_recv()
        both = num[rows, :, mine] + num_got[rows]
        if e == chips - 1:
            own[...] = both
            return
        both = both.reshape(flat, CYCLES)
        if padded > flat:
            both = jnp.concatenate([both, jnp.zeros((padded - flat, CYCLES), F32)], axis=0)
        part_out[e] = both.astype(BF16)
        copy = remote(
            part_out.at[e], part_got.at[e], p_send.at[e], p_recv.at[e], wide=place * 2 + core
        )
        copy.start()
        parts.append(copy)

    for e in range(chips):
        place = lax.rem(chip + 1 + e, chips)
        coeff = exact(weight, tab_ref[place])
        for row in range(chunk):
            wide_spec = spec[place * chunk + row].astype(F32)
            x_real, x_imag = wide_spec[:, :CYCLES], wide_spec[:, CYCLES:]
            h_real = coeff[:, row : row + 1]
            h_imag = coeff[:, 64 + row : 65 + row]
            a_real = x_real * h_real - x_imag * h_imag
            a_imag = x_real * h_imag + x_imag * h_real
            aligned = jnp.concatenate([a_real, a_imag], axis=-1).astype(BF16)
            sums = jnp.dot(picked, aligned, preferred_element_type=F32)
            num[place * chunk + row] = sums[:CLS_GRP]
        rows = pl.ds(place * chunk, chunk)
        copy = remote(
            num.at[rows, :, theirs], num_got.at[rows], n_send.at[e], n_recv.at[e], wide=sibling
        )
        copy.start()
        halves.append(copy)
        if e:
            pass_on(e - 1)
    pass_on(chips - 1)

    owner_row = owner_ref[pl.ds(col, 1), :]
    shape = (wide * 8, CLS_GRP)
    line = lax.broadcasted_iota(jnp.int32, shape, 0)
    held = (owner_row == line // 8).astype(F32)
    lower = lax.broadcasted_iota(jnp.int32, (CLS_GRP, CLS_GRP), 0)
    upper = lax.broadcasted_iota(jnp.int32, (CLS_GRP, CLS_GRP), 1)
    rank = exact(held, (lower <= upper).astype(F32)) - 1.0
    pick = held * (rank == (line % OWN_MAX).astype(F32)).astype(F32)
    early = pick * (line % 8 < OWN_MAX).astype(F32)
    late = pick - early

    peak, total = top[0:1], top[1:2]
    for d in range(1, narrow):
        tops[d - 1].wait_recv()
        other = top_got[d, 0:1]
        joined = jnp.maximum(peak, other)
        total = total * jnp.exp(peak - joined) + top_got[d, 1:2] * jnp.exp(other - joined)
        peak = joined
    ev_ref[...] = jnp.broadcast_to(peak + jnp.log(total), ev_ref.shape)
    for copy in dens:
        copy.wait_recv()
    scale = den_all[0]
    for e in range(1, chips):
        scale = scale + den_all[e]
    scale = 1.0 / (scale + TAU)
    for copy in parts:
        copy.wait_recv()
    summed = own[...].reshape(flat, CYCLES)
    for e in range(chips - 1):
        summed = summed + part_got[e].astype(F32)[:flat]
    summed = summed.reshape(chunk, CLS_GRP, CYCLES) * scale[None]
    pairs = (chunk + 1) // 2
    for pair in range(pairs):
        out = exact(early, summed[2 * pair])
        if 2 * pair + 1 < chunk:
            out = out + exact(late, summed[2 * pair + 1])
        slot_out[:, pair] = out.reshape(wide, 8, CYCLES)
    slots = []
    for d in range(1, wide):
        peer = lax.rem(me + d, wide)
        copy = remote(slot_out.at[peer], har.at[core, chip], s_send.at[d], s_recv.at[d], wide=peer)
        copy.start()
        slots.append(copy)
    har[core, chip] = slot_out[me]
    for copy in slots:
        copy.wait_recv()
    length = chips * pairs * 8
    both = jnp.concatenate(
        [har[0].reshape(length, CYCLES), har[1].reshape(length, CYCLES)], axis=1
    )
    out = exact(back_ref[...], both)
    size = OWN_MAX * ANGLES
    by_cos, by_sin = out[:size], out[size:]
    new_ref[:, :CYCLES] = (by_cos[:, :CYCLES] - by_sin[:, CYCLES:]).astype(BF16)
    new_ref[:, CYCLES:] = (by_cos[:, CYCLES:] + by_sin[:, :CYCLES]).astype(BF16)
    for copy in [den_copy] + first + second + third + halves + tops + dens + parts + slots:
        copy.wait_send()


def per_device(images, defocus, class_index, rotation_index, owner_map, roster, ref_store):
    wide = lax.axis_size("wide")
    narrow = lax.axis_size("narrow")
    chips = wide // 2
    chunk = -(-ANGLES // chips)
    pairs = (chunk + 1) // 2
    particles = images.shape[0]
    cosines, sines = tables()

    block = ref_store[0, 0]
    block_classes = block.shape[0]
    pieces_each = max(wide // (2 * block_classes), 1)
    rows = ANGLES // pieces_each
    height = up(rows, 16)
    pieces = block.reshape(block_classes, pieces_each, rows, 2, CYCLES).transpose(0, 3, 1, 2, 4)
    pieces = jnp.pad(pieces.reshape(wide, rows, CYCLES), ((0, 0), (0, height - rows), (0, 0)))

    dft = np.block([[cosines, sines], [-sines, cosines]]).astype(BF16)
    spaced = np.zeros((2 * ANGLES, 2, pieces_each, height), np.float32)
    spaced[..., :rows] = dft.astype(np.float32).reshape(2 * ANGLES, 2, pieces_each, rows)
    rdft = spaced.reshape(2 * ANGLES, -1).astype(BF16)
    turn = np.concatenate([cosines, -sines], axis=1)
    tab = np.zeros((chips, ANGLES, CYCLES), np.float32)
    back = np.zeros((2, OWN_MAX, ANGLES, chips, pairs, 2, OWN_MAX), np.float32)
    for m in range(ANGLES):
        place, row = divmod(m, chunk)
        tab[place, :, row] = cosines[:, m]
        tab[place, :, 64 + row] = sines[:, m]
        for slot in range(OWN_MAX):
            back[0, slot, :, place, row // 2, row % 2, slot] = cosines[m] / ANGLES
            back[1, slot, :, place, row // 2, row % 2, slot] = sines[m] / ANGLES
    back = back.reshape(2 * OWN_MAX * ANGLES, chips * pairs * 8)

    vmem = pl.BlockSpec(memory_space=pltpu.VMEM)
    dma = pltpu.SemaphoreType.DMA
    flat = up(chunk * CLS_GRP, 16)
    new, evidence = pl.pallas_call(
        functools.partial(kernel, wide, narrow, chunk, pieces_each),
        out_shape=(
            jax.ShapeDtypeStruct((OWN_MAX * ANGLES, 2 * CYCLES), BF16),
            jax.ShapeDtypeStruct((8, particles), F32),
        ),
        in_specs=[
            pl.BlockSpec(memory_space=pltpu.SMEM), vmem, pl.BlockSpec(memory_space=pl.ANY)
        ] + [vmem] * 9,
        out_specs=(vmem, vmem),
        scratch_shapes=[
            pltpu.VMEM((particles, ANGLES, 2 * CYCLES), BF16),
            pltpu.VMEM((chunk * chips, particles, 2 * CYCLES), BF16),
            pltpu.VMEM((wide, height, CYCLES), BF16),
            pltpu.VMEM((wide, STEPS, height, CYCLES), BF16),
            pltpu.VMEM((ANGLES, STEPS, 2 * block_classes, 2 * CYCLES), BF16),
            pltpu.VMEM((ANGLES, 2 * CLS_GRP, particles), F32),
            pltpu.VMEM((CLS_GRP, ANGLES, particles), F32),
            pltpu.VMEM((chunk * chips, CLS_GRP, 2 * CYCLES), F32),
            pltpu.VMEM((chunk * chips, CLS_GRP, CYCLES), F32),
            pltpu.VMEM((CLS_GRP, CYCLES), F32),
            pltpu.VMEM((CLS_GRP, CYCLES), F32),
            pltpu.VMEM((chips, CLS_GRP, CYCLES), F32),
            pltpu.VMEM((8, particles), F32),
            pltpu.VMEM((narrow, 8, particles), F32),
            pltpu.VMEM((chips, flat, CYCLES), BF16),
            pltpu.VMEM((chips, flat, CYCLES), BF16),
            pltpu.VMEM((chunk, CLS_GRP, CYCLES), F32),
            pltpu.VMEM((wide, pairs, 8, CYCLES), F32),
            pltpu.VMEM((2, chips, pairs, 8, CYCLES), F32),
            dma((1,)),
            dma((wide,)), dma((wide,)),
            dma((chips,)), dma((chips,)),
            dma((chips,)), dma((chips,)),
            dma((narrow,)), dma((narrow,)),
            dma((1,)), dma((1,)),
            dma((chips,)), dma((chips,)),
            dma((chips,)), dma((chips,)),
            dma((chips,)), dma((chips,)),
            dma((wide,)), dma((wide,)),
        ],
        compiler_params=pltpu.CompilerParams(
            collective_id=0, has_side_effects=True, vmem_limit_bytes=VMEM_LIMIT
        ),
        name="class_averages",
    )(
        roster, pieces, images, contrast(defocus),
        class_index.reshape(1, particles), rotation_index.reshape(1, particles),
        owner_map.reshape(narrow, CLS_GRP),
        jnp.asarray(dft), jnp.asarray(rdft), jnp.asarray(turn), jnp.asarray(tab), jnp.asarray(back),
    )
    return new.reshape(1, 1, OWN_MAX, ANGLES, 2 * CYCLES), evidence[0]


def solution(mesh):
    in_specs = (
        P("wide", None, None),
        P("wide"),
        P("wide"),
        P("wide"),
        P(),
        P(),
        P("wide", "narrow", None, None, None),
    )
    out_specs = (P("wide", "narrow", None, None, None), P("wide"))
    return jax.shard_map(
        per_device, mesh=mesh, in_specs=in_specs, out_specs=out_specs, check_vma=False
    )
```

```python
import functools
import math

import jax
import jax.numpy as jnp
import numpy as np
from jax import lax
from jax.experimental import pallas as pl
from jax.experimental.pallas import tpu as pltpu
from jax.sharding import PartitionSpec as P

CYCLES = 128
ANGLES = 72
STEPS = 3
OWN_MAX = 4
CLS_GRP = 24
SIGMA_ROT = 8
TAU = 1.0
CONTRAST = 0.1
TOP = lax.Precision.HIGHEST
MESH = pl.DeviceIdType.MESH
VMEM_LIMIT = 56 * 1024 * 1024
F32 = jnp.float32
BF16 = jnp.bfloat16
TILE = 16


def up(value, step):
    return -(-value // step) * step


def tables():
    counting = np.arange(ANGLES)
    phase = (counting[:, None] * counting[None, :] % ANGLES) * (2.0 * math.pi / ANGLES)
    return np.cos(phase).astype(np.float32), np.sin(phase).astype(np.float32)


def contrast(defocus_row):
    particles = defocus_row.shape[1]
    defocus = jnp.swapaxes(jnp.broadcast_to(defocus_row, (CYCLES, particles)), 0, 1)
    cycle = lax.broadcasted_iota(jnp.int32, (particles, CYCLES), 1).astype(F32)
    phase_angle = 8.0 * math.pi * defocus * jnp.square((cycle + 1.0) / CYCLES)
    return -jnp.sin(phase_angle) - CONTRAST * jnp.cos(phase_angle)


def high_low(value):
    high = value.astype(BF16).astype(value.dtype)
    return high, value - high


def iota(shape, dimension):
    return lax.broadcasted_iota(jnp.int32, shape, dimension)


def remote(src, dst, send_sem, recv_sem, **target):
    return pltpu.make_async_remote_copy(
        src_ref=src,
        dst_ref=dst,
        send_sem=send_sem,
        recv_sem=recv_sem,
        device_id=target,
        device_id_type=MESH,
    )


def exact(a, b):
    return jnp.dot(a, b, preferred_element_type=F32, precision=TOP)


def kernel(
    wide, narrow, chunk, pieces_each,
    roster_ref, store_ref, img_hbm, defocus_ref, class_ref, rot_ref, owner_ref,
    dft_ref, rdft_ref, turn_ref, tab_ref, back_ref,
    new_ref, ev_ref,
    piece_ref, con_ref, img_ref, spec, got, gath, rr, ct, sc, num, num_got, den, den_got, den_all, top, top_got,
    part_out, part_got, own, pick, slot_out, har,
    i_sem, a_send, a_recv, b_send, b_recv, y_send, y_recv, c_send, c_recv, t_send, t_recv, d_send, d_recv,
    e_send, e_recv, n_send, n_recv, p_send, p_recv, s_send, s_recv,
):
    me = lax.axis_index("wide")
    col = lax.axis_index("narrow")
    chips = wide // 2
    chip, core = me // 2, lax.rem(me, 2)
    sibling = chip * 2 + 1 - core
    particles = con_ref.shape[0]
    block_classes = CLS_GRP // STEPS
    load = pltpu.make_async_copy(img_hbm, img_ref, i_sem.at[0])
    load.start()
    barrier = pltpu.get_barrier_semaphore()
    for d in range(1, wide):
        pl.semaphore_signal(
            barrier, inc=1, device_id={"wide": lax.rem(me + d, wide)}, device_id_type=MESH
        )
    for d in range(1, narrow):
        pl.semaphore_signal(
            barrier, inc=1, device_id={"narrow": lax.rem(col + d, narrow)}, device_id_type=MESH
        )
    rows = ANGLES // pieces_each
    height = piece_ref.shape[1]
    for part in range(pieces_each):
        row, angle = iota((height, ANGLES), 0), iota((height, ANGLES), 1)
        take = ((row + part * rows == angle) & (row < rows)).astype(F32).astype(BF16)
        for slot in range(block_classes):
            piece = jnp.dot(take, store_ref[0, 0, slot], preferred_element_type=F32).astype(BF16)
            for half in range(2):
                piece_ref[(slot * 2 + half) * pieces_each + part] = piece[
                    :, half * CYCLES : (half + 1) * CYCLES
                ]
    pl.semaphore_wait(barrier, wide + narrow - 2)

    first = []
    for d in range(1, wide):
        peer = lax.rem(me + d, wide)
        copy = remote(piece_ref.at[peer], got.at[me], a_send.at[d], a_recv.at[d], wide=peer)
        copy.start()
        first.append(copy)
    got[me] = piece_ref[me]

    con_ref[...] = contrast(defocus_ref[...])
    class_row = lax.broadcasted_iota(jnp.int32, (CLS_GRP, particles), 0) + col * CLS_GRP
    members = (class_row == class_ref[...]).astype(F32)
    squares = jnp.square(con_ref[...])
    den[...] = exact(members, squares)
    den_copy = remote(den, den_got, d_send.at[0], d_recv.at[0], wide=sibling)
    den_copy.start()

    load.wait()
    dft = dft_ref[...]

    def spectra(group, carry):
        reals, imags = [], []
        for pair in range(TILE // 2):
            columns = []
            for which in range(2):
                row = group * TILE + pair * 2 + which
                gain = con_ref[pl.ds(row, 1), :]
                image = img_ref[row].astype(F32)
                columns.append(
                    jnp.concatenate([image[:, :CYCLES] * gain, image[:, CYCLES:] * gain], axis=0)
                )
            packed = jnp.concatenate(columns, axis=1).astype(BF16)
            out = jnp.dot(dft, packed, preferred_element_type=F32)
            for which in range(2):
                lanes = out[:, which * CYCLES : (which + 1) * CYCLES]
                reals.append(lanes[:ANGLES])
                imags.append(lanes[ANGLES:])
        rows = pl.ds(pl.multiple_of(group * TILE, TILE), TILE)
        spec[0:ANGLES, rows, 0:CYCLES] = jnp.swapaxes(jnp.stack(reals), 0, 1).astype(BF16)
        spec[0:ANGLES, rows, CYCLES:] = jnp.swapaxes(jnp.stack(imags), 0, 1).astype(BF16)
        return carry

    groups = particles // TILE
    cuts = [0, groups // 4, groups // 2, groups * 3 // 4, groups]
    lax.fori_loop(cuts[0], cuts[1], spectra, 0)
    if chunk * chips > ANGLES:
        spec[ANGLES:] = jnp.zeros((chunk * chips - ANGLES, particles, 2 * CYCLES), BF16)

    den_copy.wait_recv()
    den_all[0] = den[...] + den_got[...]
    dens = []
    for e in range(1, chips):
        peer = lax.rem(chip + e, chips) * 2 + core
        copy = remote(den_all.at[0], den_all.at[e], e_send.at[e], e_recv.at[e], wide=peer)
        copy.start()
        dens.append(copy)
    for copy in first:
        copy.wait_recv()
    for step in range(STEPS):
        gath[me, step] = got[roster_ref[col, step]]
    outer = chips // 2
    place, inner = chip // 2, lax.rem(chip, 2)
    partner = (place * 2 + 1 - inner) * 2 + core
    second, third, fourth = [], [], []
    for e in range(1, outer):
        peer = (lax.rem(place + e, outer) * 2 + inner) * 2 + core
        copy = remote(gath.at[me], gath.at[me], b_send.at[e], b_recv.at[e], wide=peer)
        copy.start()
        second.append(copy)
    lax.fori_loop(cuts[1], cuts[2], spectra, 0)
    for e in range(outer):
        origin = (lax.rem(place + outer - e, outer) * 2 + inner) * 2 + core
        if e:
            second[e - 1].wait_recv()
        piece = gath.at[origin]
        copy = remote(piece, piece, y_send.at[e], y_recv.at[e], wide=partner)
        copy.start()
        third.append(copy)
        copy = remote(piece, piece, c_send.at[e], c_recv.at[e], wide=sibling)
        copy.start()
        fourth.append(copy)
    lax.fori_loop(cuts[2], cuts[3], spectra, 0)
    for e in range(outer):
        origin = (lax.rem(place + outer - e, outer) * 2 + 1 - inner) * 2 + core
        third[e].wait_recv()
        piece = gath.at[origin]
        copy = remote(piece, piece, c_send.at[outer + e], c_recv.at[outer + e], wide=sibling)
        copy.start()
        fourth.append(copy)
    lax.fori_loop(cuts[3], cuts[4], spectra, 0)

    lanes = OWN_MAX * CLS_GRP
    classes = narrow * CLS_GRP
    source, lane = iota((classes, lanes), 0), iota((classes, lanes), 1)
    spread = (source == col * CLS_GRP + lane % CLS_GRP).astype(F32).astype(BF16)
    owner_row = jnp.broadcast_to(owner_ref[...].astype(F32), (TILE, classes)).astype(BF16)
    owner_row = jnp.dot(owner_row, spread, preferred_element_type=F32)[0:1]
    shape = (wide * TILE, lanes)
    line, lane = iota(shape, 0), iota(shape, 1)
    held = (owner_row == (line // TILE).astype(F32)).astype(F32)
    before, after = iota((lanes, lanes), 0), iota((lanes, lanes), 1)
    counted = (before <= after) & (before // CLS_GRP == after // CLS_GRP)
    rank = jnp.dot(
        held.astype(BF16), counted.astype(F32).astype(BF16), preferred_element_type=F32
    )
    wanted = (rank - 1.0 == (line % OWN_MAX).astype(F32)).astype(F32)
    wanted = wanted * (lane // CLS_GRP == line // OWN_MAX % OWN_MAX).astype(F32)
    pick[...] = (held * wanted).astype(BF16)
    for copy in fourth:
        copy.wait_recv()

    rdft = rdft_ref[...]
    power = []
    for step in range(STEPS):
        reals, imags = [], []
        for pair in range(block_classes // 2):
            columns = []
            for slot in (2 * pair, 2 * pair + 1):
                start = slot * 2 * pieces_each
                columns.append(
                    jnp.concatenate(
                        [gath[start + k, step] for k in range(2 * pieces_each)], axis=0
                    )
                )
            out = jnp.dot(rdft, jnp.concatenate(columns, axis=1), preferred_element_type=F32)
            for which in range(2):
                lanes = out[:, which * CYCLES : (which + 1) * CYCLES]
                reals.append(lanes[:ANGLES])
                imags.append(lanes[ANGLES:])
        real = jnp.swapaxes(jnp.stack(reals), 0, 1).astype(BF16).astype(F32)
        imag = jnp.swapaxes(jnp.stack(imags), 0, 1).astype(BF16).astype(F32)
        power.append(jnp.sum(real * real + imag * imag, axis=0))
        first_rows = jnp.concatenate([real, imag], axis=-1)
        second_rows = jnp.concatenate([-imag, real], axis=-1)
        rr[:, step] = jnp.concatenate([first_rows, second_rows], axis=1).astype(BF16)
    energy = lax.dot_general(
        jnp.concatenate(power, axis=0), squares, (((1,), (1,)), ((), ())),
        preferred_element_type=F32, precision=TOP,
    )

    def correlate(m, carry):
        refs = rr[m].reshape(2 * CLS_GRP, 2 * CYCLES)
        ct[m] = lax.dot_general(
            refs, spec[m], (((1,), (1,)), ((), ())), preferred_element_type=F32
        )
        return carry

    lax.fori_loop(0, ANGLES, correlate, 0, unroll=8)

    angle = lax.broadcasted_iota(jnp.int32, (ANGLES, particles), 0)
    distance = jnp.abs(angle - rot_ref[...])
    distance = jnp.minimum(distance, ANGLES - distance).astype(F32)
    prior = -0.5 * jnp.square(distance / SIGMA_ROT)
    turn = turn_ref[...]
    chosen = jnp.zeros((ANGLES, particles), F32)
    best = None
    for step in range(STEPS):
        start = step * 2 * block_classes
        real = jnp.swapaxes(ct[:, start : start + block_classes, :], 0, 1)
        imag = jnp.swapaxes(ct[:, start + block_classes : start + 2 * block_classes, :], 0, 1)
        for pair in range(block_classes // 2):
            slots = (2 * pair, 2 * pair + 1)
            both = jnp.concatenate(
                [
                    jnp.concatenate([real[s] for s in slots], axis=1),
                    jnp.concatenate([imag[s] for s in slots], axis=1),
                ],
                axis=0,
            )
            high, low = high_low(both)
            both = jnp.concatenate([high, low, high], axis=0).astype(BF16)
            turned = jnp.dot(turn, both, preferred_element_type=F32)
            for which, slot in enumerate(slots):
                c = step * block_classes + slot
                lanes = turned[:, which * particles : (which + 1) * particles]
                scores = (lanes - 0.5 * energy[c : c + 1]) / ANGLES + prior
                sc[c] = scores
                chosen = chosen + members[c : c + 1] * scores
                best = scores if best is None else jnp.maximum(best, scores)
    peak = jnp.max(best, axis=0, keepdims=True)
    total = jnp.zeros((ANGLES, particles), F32)
    for c in range(CLS_GRP):
        total = total + jnp.exp(sc[c] - peak)
    top[0:1] = peak
    top[1:2] = jnp.sum(total, axis=0, keepdims=True)
    tops = []
    for d in range(1, narrow):
        copy = remote(top, top_got.at[d], t_send.at[d], t_recv.at[d], narrow=lax.rem(col + d, narrow))
        copy.start()
        tops.append(copy)
    weight = jnp.exp(chosen - jnp.max(chosen, axis=0, keepdims=True))
    weight = weight / jnp.sum(weight, axis=0, keepdims=True)
    high, low = high_low(weight)
    weight = jnp.swapaxes(jnp.concatenate([high, high, low], axis=0), 0, 1).astype(BF16)
    picked = jnp.concatenate([members, jnp.zeros((8, particles), F32)], axis=0).astype(BF16)

    mine = pl.ds(pl.multiple_of(core * CYCLES, CYCLES), CYCLES)
    theirs = pl.ds(pl.multiple_of((1 - core) * CYCLES, CYCLES), CYCLES)
    flat = chunk * CLS_GRP
    padded = up(flat, 16)
    halves, parts = [], []

    def pass_on(e):
        place = lax.rem(chip + 1 + e, chips)
        rows = pl.ds(place * chunk, chunk)
        halves[e].wait_recv()
        both = num[rows, :, mine] + num_got[rows]
        if e == chips - 1:
            own[...] = both
            return
        both = both.reshape(flat, CYCLES)
        if padded > flat:
            both = jnp.concatenate([both, jnp.zeros((padded - flat, CYCLES), F32)], axis=0)
        part_out[e] = both.astype(BF16)
        copy = remote(
            part_out.at[e], part_got.at[e], p_send.at[e], p_recv.at[e], wide=place * 2 + core
        )
        copy.start()
        parts.append(copy)

    for e in range(chips):
        place = lax.rem(chip + 1 + e, chips)
        coeff = jnp.dot(weight, tab_ref[place], preferred_element_type=F32)
        for row in range(chunk):
            wide_spec = spec[place * chunk + row].astype(F32)
            x_real, x_imag = wide_spec[:, :CYCLES], wide_spec[:, CYCLES:]
            h_real = coeff[:, row : row + 1]
            h_imag = coeff[:, 64 + row : 65 + row]
            a_real = x_real * h_real - x_imag * h_imag
            a_imag = x_real * h_imag + x_imag * h_real
            aligned = jnp.concatenate([a_real, a_imag], axis=-1).astype(BF16)
            sums = jnp.dot(picked, aligned, preferred_element_type=F32)
            num[place * chunk + row] = sums[:CLS_GRP]
        rows = pl.ds(place * chunk, chunk)
        copy = remote(
            num.at[rows, :, theirs], num_got.at[rows], n_send.at[e], n_recv.at[e], wide=sibling
        )
        copy.start()
        halves.append(copy)
        if e:
            pass_on(e - 1)
    pass_on(chips - 1)

    peak, total = top[0:1], top[1:2]
    for d in range(1, narrow):
        tops[d - 1].wait_recv()
        other = top_got[d, 0:1]
        joined = jnp.maximum(peak, other)
        total = total * jnp.exp(peak - joined) + top_got[d, 1:2] * jnp.exp(other - joined)
        peak = joined
    ev_ref[...] = peak + jnp.log(total)
    for copy in dens:
        copy.wait_recv()
    scale = den_all[0]
    for e in range(1, chips):
        scale = scale + den_all[e]
    scale = 1.0 / (scale + TAU)
    for copy in parts:
        copy.wait_recv()
    summed = own[...].reshape(flat, CYCLES)
    for e in range(chips - 1):
        summed = summed + part_got[e].astype(F32)[:flat]
    summed = summed.reshape(chunk, CLS_GRP, CYCLES) * scale[None]
    quads = -(-chunk // OWN_MAX)
    blank = jnp.zeros((CLS_GRP, CYCLES), F32)
    for quad in range(quads):
        four = range(quad * OWN_MAX, (quad + 1) * OWN_MAX)
        four = jnp.concatenate([summed[r] if r < chunk else blank for r in four], axis=0)
        out = jnp.dot(pick[...], four.astype(BF16), preferred_element_type=F32)
        slot_out[:, quad] = out.astype(BF16).reshape(wide, TILE, CYCLES)
    slots = []
    for d in range(1, wide):
        peer = lax.rem(me + d, wide)
        copy = remote(slot_out.at[peer], har.at[core, chip], s_send.at[d], s_recv.at[d], wide=peer)
        copy.start()
        slots.append(copy)
    har[core, chip] = slot_out[me]
    for copy in slots:
        copy.wait_recv()
    length = chips * quads * TILE
    both = jnp.concatenate(
        [har[0].reshape(length, CYCLES), har[1].reshape(length, CYCLES)], axis=1
    )
    out = jnp.dot(back_ref[...], jnp.concatenate([both, both]), preferred_element_type=F32)
    size = OWN_MAX * ANGLES
    by_cos, by_sin = out[:size], out[size:]
    real = by_cos[:, :CYCLES] - by_sin[:, CYCLES:]
    imag = by_cos[:, CYCLES:] + by_sin[:, :CYCLES]
    for slot in range(OWN_MAX):
        span = slice(slot * ANGLES, (slot + 1) * ANGLES)
        new_ref[0, 0, slot, :, :CYCLES] = real[span].astype(BF16)
        new_ref[0, 0, slot, :, CYCLES:] = imag[span].astype(BF16)
    for copy in [den_copy] + first + second + third + fourth + halves + tops + dens + parts + slots:
        copy.wait_send()


def per_device(images, defocus, class_index, rotation_index, owner_map, roster, ref_store):
    wide = lax.axis_size("wide")
    narrow = lax.axis_size("narrow")
    chips = wide // 2
    chunk = -(-ANGLES // chips)
    quads = -(-chunk // OWN_MAX)
    particles = images.shape[0]
    cosines, sines = tables()

    block_classes = ref_store.shape[2]
    pieces_each = max(wide // (2 * block_classes), 1)
    rows = ANGLES // pieces_each
    height = up(rows, 16)

    dft = np.block([[cosines, sines], [-sines, cosines]]).astype(BF16)
    spaced = np.zeros((2 * ANGLES, 2, pieces_each, height), np.float32)
    spaced[..., :rows] = dft.astype(np.float32).reshape(2 * ANGLES, 2, pieces_each, rows)
    rdft = spaced.reshape(2 * ANGLES, -1).astype(BF16)
    turn = np.concatenate([cosines, -sines], axis=1)
    tab = np.zeros((chips, ANGLES, CYCLES), np.float32)
    back = np.zeros((2, OWN_MAX, ANGLES, chips, quads, OWN_MAX, OWN_MAX), np.float32)
    for m in range(ANGLES):
        place, row = divmod(m, chunk)
        tab[place, :, row] = cosines[:, m]
        tab[place, :, 64 + row] = sines[:, m]
        for slot in range(OWN_MAX):
            back[0, slot, :, place, row // OWN_MAX, row % OWN_MAX, slot] = cosines[m] / ANGLES
            back[1, slot, :, place, row // OWN_MAX, row % OWN_MAX, slot] = sines[m] / ANGLES
    back = back.reshape(2 * OWN_MAX * ANGLES, chips * quads * TILE)
    high, low = high_low(back)
    back = np.concatenate([high, low], axis=1).astype(BF16)
    high, low = high_low(turn)
    turn = np.concatenate([high, high, low], axis=1).astype(BF16)
    high, low = high_low(tab)
    tab = np.concatenate([high, low, high], axis=1).astype(BF16)

    vmem = pl.BlockSpec(memory_space=pltpu.VMEM)
    dma = pltpu.SemaphoreType.DMA
    flat = up(chunk * CLS_GRP, 16)
    new, evidence = pl.pallas_call(
        functools.partial(kernel, wide, narrow, chunk, pieces_each),
        out_shape=(
            jax.ShapeDtypeStruct((1, 1, OWN_MAX, ANGLES, 2 * CYCLES), BF16),
            jax.ShapeDtypeStruct((1, particles), F32),
        ),
        in_specs=[
            pl.BlockSpec(memory_space=pltpu.SMEM), vmem, pl.BlockSpec(memory_space=pl.ANY)
        ] + [vmem] * 9,
        out_specs=(vmem, vmem),
        scratch_shapes=[
            pltpu.VMEM((wide, height, CYCLES), BF16),
            pltpu.VMEM((particles, CYCLES), F32),
            pltpu.VMEM((particles, ANGLES, 2 * CYCLES), BF16),
            pltpu.VMEM((chunk * chips, particles, 2 * CYCLES), BF16),
            pltpu.VMEM((wide, height, CYCLES), BF16),
            pltpu.VMEM((wide, STEPS, height, CYCLES), BF16),
            pltpu.VMEM((ANGLES, STEPS, 2 * block_classes, 2 * CYCLES), BF16),
            pltpu.VMEM((ANGLES, 2 * CLS_GRP, particles), F32),
            pltpu.VMEM((CLS_GRP, ANGLES, particles), F32),
            pltpu.VMEM((chunk * chips, CLS_GRP, 2 * CYCLES), F32),
            pltpu.VMEM((chunk * chips, CLS_GRP, CYCLES), F32),
            pltpu.VMEM((CLS_GRP, CYCLES), F32),
            pltpu.VMEM((CLS_GRP, CYCLES), F32),
            pltpu.VMEM((chips, CLS_GRP, CYCLES), F32),
            pltpu.VMEM((8, particles), F32),
            pltpu.VMEM((narrow, 8, particles), F32),
            pltpu.VMEM((chips, flat, CYCLES), BF16),
            pltpu.VMEM((chips, flat, CYCLES), BF16),
            pltpu.VMEM((chunk, CLS_GRP, CYCLES), F32),
            pltpu.VMEM((wide * TILE, OWN_MAX * CLS_GRP), BF16),
            pltpu.VMEM((wide, quads, TILE, CYCLES), BF16),
            pltpu.VMEM((2, chips, quads, TILE, CYCLES), BF16),
            dma((1,)),
            dma((wide,)), dma((wide,)),
            dma((chips,)), dma((chips,)),
            dma((chips,)), dma((chips,)),
            dma((chips,)), dma((chips,)),
            dma((narrow,)), dma((narrow,)),
            dma((1,)), dma((1,)),
            dma((chips,)), dma((chips,)),
            dma((chips,)), dma((chips,)),
            dma((chips,)), dma((chips,)),
            dma((wide,)), dma((wide,)),
        ],
        compiler_params=pltpu.CompilerParams(
            collective_id=0, has_side_effects=True, vmem_limit_bytes=VMEM_LIMIT
        ),
        name="class_averages",
    )(
        roster, ref_store, images, defocus.reshape(1, particles),
        class_index.reshape(1, particles), rotation_index.reshape(1, particles),
        owner_map.reshape(1, narrow * CLS_GRP),
        jnp.asarray(dft), jnp.asarray(rdft), jnp.asarray(turn), jnp.asarray(tab), jnp.asarray(back),
    )
    return new, evidence.reshape(particles)


def solution(mesh):
    in_specs = (
        P("wide", None, None),
        P("wide"),
        P("wide"),
        P("wide"),
        P(),
        P(),
        P("wide", "narrow", None, None, None),
    )
    out_specs = (P("wide", "narrow", None, None, None), P("wide"))
    return jax.shard_map(
        per_device, mesh=mesh, in_specs=in_specs, out_specs=out_specs, check_vma=False
    )
```

```python
import functools
import math

import jax
import jax.numpy as jnp
import numpy as np
from jax import lax
from jax.experimental import pallas as pl
from jax.experimental.pallas import tpu as pltpu
from jax.sharding import PartitionSpec as P

CYCLES = 128
ANGLES = 72
STEPS = 3
OWN_MAX = 4
CLS_GRP = 24
SIGMA_ROT = 8
TAU = 1.0
CONTRAST = 0.1
TOP = lax.Precision.HIGHEST
MESH = pl.DeviceIdType.MESH
VMEM_LIMIT = 56 * 1024 * 1024
F32 = jnp.float32
BF16 = jnp.bfloat16
TILE = 16


def up(value, step):
    return -(-value // step) * step


def tables():
    counting = np.arange(ANGLES)
    phase = (counting[:, None] * counting[None, :] % ANGLES) * (2.0 * math.pi / ANGLES)
    return np.cos(phase).astype(np.float32), np.sin(phase).astype(np.float32)


def contrast(defocus_row):
    particles = defocus_row.shape[1]
    defocus = jnp.swapaxes(jnp.broadcast_to(defocus_row, (CYCLES, particles)), 0, 1)
    cycle = lax.broadcasted_iota(jnp.int32, (particles, CYCLES), 1).astype(F32)
    phase_angle = 8.0 * math.pi * defocus * jnp.square((cycle + 1.0) / CYCLES)
    return -jnp.sin(phase_angle) - CONTRAST * jnp.cos(phase_angle)


def high_low(value):
    high = value.astype(BF16).astype(value.dtype)
    return high, value - high


def iota(shape, dimension):
    return lax.broadcasted_iota(jnp.int32, shape, dimension)


def remote(src, dst, send_sem, recv_sem, **target):
    return pltpu.make_async_remote_copy(
        src_ref=src,
        dst_ref=dst,
        send_sem=send_sem,
        recv_sem=recv_sem,
        device_id=target,
        device_id_type=MESH,
    )


def exact(a, b):
    return jnp.dot(a, b, preferred_element_type=F32, precision=TOP)


def kernel(
    wide, narrow, chunk, pieces_each,
    roster_ref, store_ref, img_hbm, defocus_ref, class_ref, rot_ref, owner_ref,
    dft_ref, rdft_ref, turn_ref, tab_ref, back_ref,
    new_ref, peak_ref, total_ref,
    piece_ref, con_ref, img_ref, spec, spec_t, coeffs, got, gath, rr, ct, sc, num, num_got, den, den_got, den_all, top, top_got,
    part_out, part_got, own, pick, slot_out, har,
    i_sem, a_send, a_recv, b_send, b_recv, y_send, y_recv, c_send, c_recv, t_send, t_recv, d_send, d_recv,
    e_send, e_recv, n_send, n_recv, p_send, p_recv, s_send, s_recv,
):
    me = lax.axis_index("wide")
    col = lax.axis_index("narrow")
    chips = wide // 2
    chip, core = me // 2, lax.rem(me, 2)
    sibling = chip * 2 + 1 - core
    particles = con_ref.shape[0]
    block_classes = CLS_GRP // STEPS
    load = pltpu.make_async_copy(img_hbm, img_ref, i_sem.at[0])
    load.start()
    barrier = pltpu.get_barrier_semaphore()
    for d in range(1, wide):
        pl.semaphore_signal(
            barrier, inc=1, device_id={"wide": lax.rem(me + d, wide)}, device_id_type=MESH
        )
    for d in range(1, narrow):
        pl.semaphore_signal(
            barrier, inc=1, device_id={"narrow": lax.rem(col + d, narrow)}, device_id_type=MESH
        )
    rows = ANGLES // pieces_each
    height = piece_ref.shape[1]
    for part in range(pieces_each):
        row, angle = iota((height, ANGLES), 0), iota((height, ANGLES), 1)
        take = ((row + part * rows == angle) & (row < rows)).astype(F32).astype(BF16)
        for slot in range(block_classes):
            piece = jnp.dot(take, store_ref[0, 0, slot], preferred_element_type=F32).astype(BF16)
            for half in range(2):
                piece_ref[(slot * 2 + half) * pieces_each + part] = piece[
                    :, half * CYCLES : (half + 1) * CYCLES
                ]
    pl.semaphore_wait(barrier, wide + narrow - 2)

    first = []
    for d in range(1, wide):
        peer = lax.rem(me + d, wide)
        copy = remote(piece_ref.at[peer], got.at[me], a_send.at[d], a_recv.at[d], wide=peer)
        copy.start()
        first.append(copy)
    got[me] = piece_ref[me]

    con_ref[...] = contrast(defocus_ref[...])
    class_row = lax.broadcasted_iota(jnp.int32, (CLS_GRP, particles), 0) + col * CLS_GRP
    members = (class_row == class_ref[...]).astype(F32)
    squares = jnp.square(con_ref[...])
    den[...] = exact(members, squares)
    den_copy = remote(den, den_got, d_send.at[0], d_recv.at[0], wide=sibling)
    den_copy.start()

    load.wait()
    dft = dft_ref[...]

    def spectra(group, carry):
        reals, imags = [], []
        for pair in range(TILE // 2):
            columns = []
            for which in range(2):
                row = group * TILE + pair * 2 + which
                gain = con_ref[pl.ds(row, 1), :]
                image = img_ref[row].astype(F32)
                columns.append(
                    jnp.concatenate([image[:, :CYCLES] * gain, image[:, CYCLES:] * gain], axis=0)
                )
            packed = jnp.concatenate(columns, axis=1).astype(BF16)
            out = jnp.dot(dft, packed, preferred_element_type=F32)
            for which in range(2):
                lanes = out[:, which * CYCLES : (which + 1) * CYCLES]
                reals.append(lanes[:ANGLES])
                imags.append(lanes[ANGLES:])
        rows = pl.ds(pl.multiple_of(group * TILE, TILE), TILE)
        spec[0:ANGLES, rows, 0:CYCLES] = jnp.swapaxes(jnp.stack(reals), 0, 1).astype(BF16)
        spec[0:ANGLES, rows, CYCLES:] = jnp.swapaxes(jnp.stack(imags), 0, 1).astype(BF16)
        return carry

    groups = particles // TILE
    cuts = [0, groups // 4, groups // 2, groups * 3 // 4, groups]
    lax.fori_loop(cuts[0], cuts[1], spectra, 0)
    if chunk * chips > ANGLES:
        spec[ANGLES:] = jnp.zeros((chunk * chips - ANGLES, particles, 2 * CYCLES), BF16)

    den_copy.wait_recv()
    den_all[0] = den[...] + den_got[...]
    dens = []
    for e in range(1, chips):
        peer = lax.rem(chip + e, chips) * 2 + core
        copy = remote(den_all.at[0], den_all.at[e], e_send.at[e], e_recv.at[e], wide=peer)
        copy.start()
        dens.append(copy)
    for copy in first:
        copy.wait_recv()
    for step in range(STEPS):
        gath[me, step] = got[roster_ref[col, step]]
    outer = chips // 2
    place, inner = chip // 2, lax.rem(chip, 2)
    partner = (place * 2 + 1 - inner) * 2 + core
    second, third, fourth = [], [], []
    for e in range(1, outer):
        peer = (lax.rem(place + e, outer) * 2 + inner) * 2 + core
        copy = remote(gath.at[me], gath.at[me], b_send.at[e], b_recv.at[e], wide=peer)
        copy.start()
        second.append(copy)
    lax.fori_loop(cuts[1], cuts[2], spectra, 0)
    for e in range(outer):
        origin = (lax.rem(place + outer - e, outer) * 2 + inner) * 2 + core
        if e:
            second[e - 1].wait_recv()
        piece = gath.at[origin]
        copy = remote(piece, piece, y_send.at[e], y_recv.at[e], wide=partner)
        copy.start()
        third.append(copy)
        copy = remote(piece, piece, c_send.at[e], c_recv.at[e], wide=sibling)
        copy.start()
        fourth.append(copy)
    lax.fori_loop(cuts[2], cuts[3], spectra, 0)
    for e in range(outer):
        origin = (lax.rem(place + outer - e, outer) * 2 + 1 - inner) * 2 + core
        third[e].wait_recv()
        piece = gath.at[origin]
        copy = remote(piece, piece, c_send.at[outer + e], c_recv.at[outer + e], wide=sibling)
        copy.start()
        fourth.append(copy)
    lax.fori_loop(cuts[3], cuts[4], spectra, 0)

    lanes = OWN_MAX * CLS_GRP
    classes = narrow * CLS_GRP
    source, lane = iota((classes, lanes), 0), iota((classes, lanes), 1)
    spread = (source == col * CLS_GRP + lane % CLS_GRP).astype(F32).astype(BF16)
    owner_row = jnp.broadcast_to(owner_ref[...].astype(F32), (TILE, classes)).astype(BF16)
    owner_row = jnp.dot(owner_row, spread, preferred_element_type=F32)[0:1]
    shape = (wide * TILE, lanes)
    line, lane = iota(shape, 0), iota(shape, 1)
    held = (owner_row == (line // TILE).astype(F32)).astype(F32)
    before, after = iota((lanes, lanes), 0), iota((lanes, lanes), 1)
    counted = (before <= after) & (before // CLS_GRP == after // CLS_GRP)
    rank = jnp.dot(
        held.astype(BF16), counted.astype(F32).astype(BF16), preferred_element_type=F32
    )
    wanted = (rank - 1.0 == (line % OWN_MAX).astype(F32)).astype(F32)
    wanted = wanted * (lane // CLS_GRP == line // OWN_MAX % OWN_MAX).astype(F32)
    pick[...] = (held * wanted).astype(BF16)

    def flip(m, carry):
        spec_t[m] = jnp.swapaxes(spec[m], 0, 1)
        return carry

    lax.fori_loop(0, ANGLES, flip, 0, unroll=4)
    for copy in fourth:
        copy.wait_recv()

    rdft = rdft_ref[...]
    power = []
    for step in range(STEPS):
        reals, imags = [], []
        for pair in range(block_classes // 2):
            columns = []
            for slot in (2 * pair, 2 * pair + 1):
                start = slot * 2 * pieces_each
                columns.append(
                    jnp.concatenate(
                        [gath[start + k, step] for k in range(2 * pieces_each)], axis=0
                    )
                )
            out = jnp.dot(rdft, jnp.concatenate(columns, axis=1), preferred_element_type=F32)
            for which in range(2):
                lanes = out[:, which * CYCLES : (which + 1) * CYCLES]
                reals.append(lanes[:ANGLES])
                imags.append(lanes[ANGLES:])
        real = jnp.swapaxes(jnp.stack(reals), 0, 1).astype(BF16).astype(F32)
        imag = jnp.swapaxes(jnp.stack(imags), 0, 1).astype(BF16).astype(F32)
        power.append(jnp.sum(real * real + imag * imag, axis=0))
        first_rows = jnp.concatenate([real, imag], axis=-1)
        second_rows = jnp.concatenate([-imag, real], axis=-1)
        rr[:, step] = jnp.concatenate([first_rows, second_rows], axis=1).astype(BF16)
    energy = lax.dot_general(
        jnp.concatenate(power, axis=0), squares, (((1,), (1,)), ((), ())),
        preferred_element_type=F32, precision=TOP,
    )

    def correlate(m, carry):
        refs = rr[m].reshape(2 * CLS_GRP, 2 * CYCLES)
        ct[m] = jnp.dot(refs, spec_t[m], preferred_element_type=F32)
        return carry

    lax.fori_loop(0, ANGLES, correlate, 0, unroll=8)

    angle = lax.broadcasted_iota(jnp.int32, (ANGLES, particles), 0)
    distance = jnp.abs(angle - rot_ref[...])
    distance = jnp.minimum(distance, ANGLES - distance).astype(F32)
    prior = -0.5 * jnp.square(distance / SIGMA_ROT)
    turn = turn_ref[...]
    chosen = jnp.zeros((ANGLES, particles), F32)
    best = None
    for step in range(STEPS):
        start = step * 2 * block_classes
        real = jnp.swapaxes(ct[:, start : start + block_classes, :], 0, 1)
        imag = jnp.swapaxes(ct[:, start + block_classes : start + 2 * block_classes, :], 0, 1)
        for pair in range(block_classes // 2):
            slots = (2 * pair, 2 * pair + 1)
            both = jnp.concatenate(
                [
                    jnp.concatenate([real[s] for s in slots], axis=1),
                    jnp.concatenate([imag[s] for s in slots], axis=1),
                ],
                axis=0,
            )
            high, low = high_low(both)
            both = jnp.concatenate([high, low, high], axis=0).astype(BF16)
            turned = jnp.dot(turn, both, preferred_element_type=F32)
            for which, slot in enumerate(slots):
                c = step * block_classes + slot
                lanes = turned[:, which * particles : (which + 1) * particles]
                scores = (lanes - 0.5 * energy[c : c + 1]) / ANGLES + prior
                sc[c] = scores
                chosen = chosen + members[c : c + 1] * scores
                best = scores if best is None else jnp.maximum(best, scores)
    peak = jnp.max(best, axis=0, keepdims=True)
    total = jnp.zeros((ANGLES, particles), F32)
    for c in range(CLS_GRP):
        total = total + jnp.exp(sc[c] - peak)
    top[0:1] = peak
    top[1:2] = jnp.sum(total, axis=0, keepdims=True)
    tops = []
    for d in range(1, narrow):
        copy = remote(top, top_got.at[d], t_send.at[d], t_recv.at[d], narrow=lax.rem(col + d, narrow))
        copy.start()
        tops.append(copy)
    weight = jnp.exp(chosen - jnp.max(chosen, axis=0, keepdims=True))
    weight = weight / jnp.sum(weight, axis=0, keepdims=True)
    high, low = high_low(weight)
    weight = jnp.swapaxes(jnp.concatenate([high, high, low], axis=0), 0, 1).astype(BF16)
    coeff = jnp.dot(weight, tab_ref[...], preferred_element_type=F32)
    for place in range(chips):
        coeffs[place] = coeff[:, place * CYCLES : (place + 1) * CYCLES]
    picked = jnp.concatenate([members, jnp.zeros((8, particles), F32)], axis=0).astype(BF16)

    mine = pl.ds(pl.multiple_of(core * CYCLES, CYCLES), CYCLES)
    theirs = pl.ds(pl.multiple_of((1 - core) * CYCLES, CYCLES), CYCLES)
    flat = chunk * CLS_GRP
    padded = up(flat, 16)
    halves, parts = [], []

    def pass_on(e):
        place = lax.rem(chip + 1 + e, chips)
        rows = pl.ds(place * chunk, chunk)
        halves[e].wait_recv()
        both = num[rows, :, mine] + num_got[rows]
        if e == chips - 1:
            own[...] = both
            return
        both = both.reshape(flat, CYCLES)
        if padded > flat:
            both = jnp.concatenate([both, jnp.zeros((padded - flat, CYCLES), F32)], axis=0)
        part_out[e] = both.astype(BF16)
        copy = remote(
            part_out.at[e], part_got.at[e], p_send.at[e], p_recv.at[e], wide=place * 2 + core
        )
        copy.start()
        parts.append(copy)

    for e in range(chips):
        place = lax.rem(chip + 1 + e, chips)
        coeff = coeffs[place]
        for row in range(chunk):
            wide_spec = spec[place * chunk + row].astype(F32)
            x_real, x_imag = wide_spec[:, :CYCLES], wide_spec[:, CYCLES:]
            h_real = coeff[:, row : row + 1]
            h_imag = coeff[:, 64 + row : 65 + row]
            a_real = x_real * h_real - x_imag * h_imag
            a_imag = x_real * h_imag + x_imag * h_real
            aligned = jnp.concatenate([a_real, a_imag], axis=-1).astype(BF16)
            sums = jnp.dot(picked, aligned, preferred_element_type=F32)
            num[place * chunk + row] = sums[:CLS_GRP]
        rows = pl.ds(place * chunk, chunk)
        copy = remote(
            num.at[rows, :, theirs], num_got.at[rows], n_send.at[e], n_recv.at[e], wide=sibling
        )
        copy.start()
        halves.append(copy)
        if e:
            pass_on(e - 1)
    pass_on(chips - 1)

    peak, total = top[0:1], top[1:2]
    for d in range(1, narrow):
        tops[d - 1].wait_recv()
        other = top_got[d, 0:1]
        joined = jnp.maximum(peak, other)
        total = total * jnp.exp(peak - joined) + top_got[d, 1:2] * jnp.exp(other - joined)
        peak = joined
    peak_ref[...] = peak
    total_ref[...] = total
    for copy in dens:
        copy.wait_recv()
    scale = den_all[0]
    for e in range(1, chips):
        scale = scale + den_all[e]
    scale = 1.0 / (scale + TAU)
    for copy in parts:
        copy.wait_recv()
    summed = own[...].reshape(flat, CYCLES)
    for e in range(chips - 1):
        summed = summed + part_got[e].astype(F32)[:flat]
    summed = summed.reshape(chunk, CLS_GRP, CYCLES) * scale[None]
    quads = -(-chunk // OWN_MAX)
    blank = jnp.zeros((CLS_GRP, CYCLES), F32)
    for quad in range(quads):
        four = range(quad * OWN_MAX, (quad + 1) * OWN_MAX)
        four = jnp.concatenate([summed[r] if r < chunk else blank for r in four], axis=0)
        out = jnp.dot(pick[...], four.astype(BF16), preferred_element_type=F32)
        slot_out[:, quad] = out.astype(BF16).reshape(wide, TILE, CYCLES)
    slots = []
    for d in range(1, wide):
        peer = lax.rem(me + d, wide)
        copy = remote(slot_out.at[peer], har.at[core, chip], s_send.at[d], s_recv.at[d], wide=peer)
        copy.start()
        slots.append(copy)
    har[core, chip] = slot_out[me]
    for copy in slots:
        copy.wait_recv()
    length = chips * quads * TILE
    both = jnp.concatenate(
        [har[0].reshape(length, CYCLES), har[1].reshape(length, CYCLES)], axis=1
    )
    out = jnp.dot(back_ref[...], jnp.concatenate([both, both]), preferred_element_type=F32)
    size = OWN_MAX * ANGLES
    by_cos, by_sin = out[:size], out[size:]
    real = by_cos[:, :CYCLES] - by_sin[:, CYCLES:]
    imag = by_cos[:, CYCLES:] + by_sin[:, :CYCLES]
    for slot in range(OWN_MAX):
        span = slice(slot * ANGLES, (slot + 1) * ANGLES)
        new_ref[0, 0, slot, :, :CYCLES] = real[span]
        new_ref[0, 0, slot, :, CYCLES:] = imag[span]
    for copy in [den_copy] + first + second + third + fourth + halves + tops + dens + parts + slots:
        copy.wait_send()


def per_device(images, defocus, class_index, rotation_index, owner_map, roster, ref_store):
    wide = lax.axis_size("wide")
    narrow = lax.axis_size("narrow")
    chips = wide // 2
    chunk = -(-ANGLES // chips)
    quads = -(-chunk // OWN_MAX)
    particles = images.shape[0]
    cosines, sines = tables()

    block_classes = ref_store.shape[2]
    pieces_each = max(wide // (2 * block_classes), 1)
    rows = ANGLES // pieces_each
    height = up(rows, 16)

    dft = np.block([[cosines, sines], [-sines, cosines]]).astype(BF16)
    spaced = np.zeros((2 * ANGLES, 2, pieces_each, height), np.float32)
    spaced[..., :rows] = dft.astype(np.float32).reshape(2 * ANGLES, 2, pieces_each, rows)
    rdft = spaced.reshape(2 * ANGLES, -1).astype(BF16)
    turn = np.concatenate([cosines, -sines], axis=1)
    tab = np.zeros((chips, ANGLES, CYCLES), np.float32)
    back = np.zeros((2, OWN_MAX, ANGLES, chips, quads, OWN_MAX, OWN_MAX), np.float32)
    for m in range(ANGLES):
        place, row = divmod(m, chunk)
        tab[place, :, row] = cosines[:, m]
        tab[place, :, 64 + row] = sines[:, m]
        for slot in range(OWN_MAX):
            back[0, slot, :, place, row // OWN_MAX, row % OWN_MAX, slot] = cosines[m] / ANGLES
            back[1, slot, :, place, row // OWN_MAX, row % OWN_MAX, slot] = sines[m] / ANGLES
    back = back.reshape(2 * OWN_MAX * ANGLES, chips * quads * TILE)
    high, low = high_low(back)
    back = np.concatenate([high, low], axis=1).astype(BF16)
    high, low = high_low(turn)
    turn = np.concatenate([high, high, low], axis=1).astype(BF16)
    high, low = high_low(tab)
    tab = np.concatenate([high, low, high], axis=1).transpose(1, 0, 2).reshape(3 * ANGLES, -1)
    tab = tab.astype(BF16)

    vmem = pl.BlockSpec(memory_space=pltpu.VMEM)
    dma = pltpu.SemaphoreType.DMA
    flat = up(chunk * CLS_GRP, 16)
    new, peak, total = pl.pallas_call(
        functools.partial(kernel, wide, narrow, chunk, pieces_each),
        out_shape=(
            jax.ShapeDtypeStruct((1, 1, OWN_MAX, ANGLES, 2 * CYCLES), F32),
            jax.ShapeDtypeStruct((1, particles), F32),
            jax.ShapeDtypeStruct((1, particles), F32),
        ),
        in_specs=[
            pl.BlockSpec(memory_space=pltpu.SMEM), vmem, pl.BlockSpec(memory_space=pl.ANY)
        ] + [vmem] * 9,
        out_specs=(vmem, vmem, vmem),
        scratch_shapes=[
            pltpu.VMEM((wide, height, CYCLES), BF16),
            pltpu.VMEM((particles, CYCLES), F32),
            pltpu.VMEM((particles, ANGLES, 2 * CYCLES), BF16),
            pltpu.VMEM((chunk * chips, particles, 2 * CYCLES), BF16),
            pltpu.VMEM((ANGLES, 2 * CYCLES, particles), BF16),
            pltpu.VMEM((chips, particles, CYCLES), F32),
            pltpu.VMEM((wide, height, CYCLES), BF16),
            pltpu.VMEM((wide, STEPS, height, CYCLES), BF16),
            pltpu.VMEM((ANGLES, STEPS, 2 * block_classes, 2 * CYCLES), BF16),
            pltpu.VMEM((ANGLES, 2 * CLS_GRP, particles), F32),
            pltpu.VMEM((CLS_GRP, ANGLES, particles), F32),
            pltpu.VMEM((chunk * chips, CLS_GRP, 2 * CYCLES), F32),
            pltpu.VMEM((chunk * chips, CLS_GRP, CYCLES), F32),
            pltpu.VMEM((CLS_GRP, CYCLES), F32),
            pltpu.VMEM((CLS_GRP, CYCLES), F32),
            pltpu.VMEM((chips, CLS_GRP, CYCLES), F32),
            pltpu.VMEM((8, particles), F32),
            pltpu.VMEM((narrow, 8, particles), F32),
            pltpu.VMEM((chips, flat, CYCLES), BF16),
            pltpu.VMEM((chips, flat, CYCLES), BF16),
            pltpu.VMEM((chunk, CLS_GRP, CYCLES), F32),
            pltpu.VMEM((wide * TILE, OWN_MAX * CLS_GRP), BF16),
            pltpu.VMEM((wide, quads, TILE, CYCLES), BF16),
            pltpu.VMEM((2, chips, quads, TILE, CYCLES), BF16),
            dma((1,)),
            dma((wide,)), dma((wide,)),
            dma((chips,)), dma((chips,)),
            dma((chips,)), dma((chips,)),
            dma((chips,)), dma((chips,)),
            dma((narrow,)), dma((narrow,)),
            dma((1,)), dma((1,)),
            dma((chips,)), dma((chips,)),
            dma((chips,)), dma((chips,)),
            dma((chips,)), dma((chips,)),
            dma((wide,)), dma((wide,)),
        ],
        compiler_params=pltpu.CompilerParams(
            collective_id=0, has_side_effects=True, vmem_limit_bytes=VMEM_LIMIT
        ),
        name="class_averages",
    )(
        roster, ref_store, images, defocus.reshape(1, particles),
        class_index.reshape(1, particles), rotation_index.reshape(1, particles),
        owner_map.reshape(1, narrow * CLS_GRP),
        jnp.asarray(dft), jnp.asarray(rdft), jnp.asarray(turn), jnp.asarray(tab), jnp.asarray(back),
    )
    return new.astype(BF16), (peak + jnp.log(total)).reshape(particles)


def solution(mesh):
    in_specs = (
        P("wide", None, None),
        P("wide"),
        P("wide"),
        P("wide"),
        P(),
        P(),
        P("wide", "narrow", None, None, None),
    )
    out_specs = (P("wide", "narrow", None, None, None), P("wide"))
    return jax.shard_map(
        per_device, mesh=mesh, in_specs=in_specs, out_specs=out_specs, check_vma=False
    )
```

```python
import functools
import math

import jax
import jax.numpy as jnp
import numpy as np
from jax import lax
from jax.experimental import pallas as pl
from jax.experimental.pallas import tpu as pltpu
from jax.sharding import PartitionSpec as P

CYCLES = 128
ANGLES = 72
STEPS = 3
OWN_MAX = 4
CLS_GRP = 24
SIGMA_ROT = 8
TAU = 1.0
CONTRAST = 0.1
TOP = lax.Precision.HIGHEST
MESH = pl.DeviceIdType.MESH
VMEM_LIMIT = 56 * 1024 * 1024
F32 = jnp.float32
BF16 = jnp.bfloat16
TILE = 16


def up(value, step):
    return -(-value // step) * step


def tables():
    counting = np.arange(ANGLES)
    phase = (counting[:, None] * counting[None, :] % ANGLES) * (2.0 * math.pi / ANGLES)
    return np.cos(phase).astype(np.float32), np.sin(phase).astype(np.float32)


def contrast(defocus_row):
    particles = defocus_row.shape[1]
    defocus = jnp.swapaxes(jnp.broadcast_to(defocus_row, (CYCLES, particles)), 0, 1)
    cycle = lax.broadcasted_iota(jnp.int32, (particles, CYCLES), 1).astype(F32)
    phase_angle = 8.0 * math.pi * defocus * jnp.square((cycle + 1.0) / CYCLES)
    return -jnp.sin(phase_angle) - CONTRAST * jnp.cos(phase_angle)


def high_low(value):
    high = value.astype(BF16).astype(value.dtype)
    return high, value - high


def iota(shape, dimension):
    return lax.broadcasted_iota(jnp.int32, shape, dimension)


def remote(src, dst, send_sem, recv_sem, **target):
    return pltpu.make_async_remote_copy(
        src_ref=src,
        dst_ref=dst,
        send_sem=send_sem,
        recv_sem=recv_sem,
        device_id=target,
        device_id_type=MESH,
    )


def exact(a, b):
    return jnp.dot(a, b, preferred_element_type=F32, precision=TOP)


def kernel(
    wide, narrow, chunk, pieces_each,
    roster_ref, store_ref, img_hbm, defocus_ref, class_ref, rot_ref, owner_ref,
    dft_ref, rdft_ref, turn_ref, tab_ref, back_ref,
    new_ref, ev_ref,
    piece_ref, con_ref, img_ref, spec_re, spec_im, coeffs, got, gath, rr_a, rr_b, ct, sc, num, num_got, den, den_got, den_all, top, top_got,
    part_out, part_got, own, pick, slot_out, har,
    i_sem, a_send, a_recv, b_send, b_recv, y_send, y_recv, c_send, c_recv, t_send, t_recv, d_send, d_recv,
    e_send, e_recv, n_send, n_recv, p_send, p_recv, s_send, s_recv,
):
    me = lax.axis_index("wide")
    col = lax.axis_index("narrow")
    chips = wide // 2
    chip, core = me // 2, lax.rem(me, 2)
    sibling = chip * 2 + 1 - core
    particles = con_ref.shape[0]
    pitch = particles + 8
    row_pitch = 2 * CLS_GRP + 8
    block_classes = CLS_GRP // STEPS
    load = pltpu.make_async_copy(img_hbm, img_ref, i_sem.at[0])
    load.start()
    barrier = pltpu.get_barrier_semaphore()
    for d in range(1, wide):
        pl.semaphore_signal(
            barrier, inc=1, device_id={"wide": lax.rem(me + d, wide)}, device_id_type=MESH
        )
    for d in range(1, narrow):
        pl.semaphore_signal(
            barrier, inc=1, device_id={"narrow": lax.rem(col + d, narrow)}, device_id_type=MESH
        )
    rows = ANGLES // pieces_each
    height = piece_ref.shape[1]
    for part in range(pieces_each):
        row, angle = iota((height, ANGLES), 0), iota((height, ANGLES), 1)
        take = ((row + part * rows == angle) & (row < rows)).astype(F32).astype(BF16)
        for slot in range(block_classes):
            piece = jnp.dot(take, store_ref[0, 0, slot], preferred_element_type=F32).astype(BF16)
            for half in range(2):
                piece_ref[(slot * 2 + half) * pieces_each + part] = piece[
                    :, half * CYCLES : (half + 1) * CYCLES
                ]
    pl.semaphore_wait(barrier, wide + narrow - 2)

    first = []
    for d in range(1, wide):
        peer = lax.rem(me + d, wide)
        copy = remote(piece_ref.at[peer], got.at[me], a_send.at[d], a_recv.at[d], wide=peer)
        copy.start()
        first.append(copy)
    got[me] = piece_ref[me]

    con_ref[...] = contrast(defocus_ref[...])
    class_row = lax.broadcasted_iota(jnp.int32, (CLS_GRP, particles), 0) + col * CLS_GRP
    members = (class_row == class_ref[...]).astype(F32)
    squares = jnp.square(con_ref[...])
    den[...] = exact(members, squares)
    den_copy = remote(den, den_got, d_send.at[0], d_recv.at[0], wide=sibling)
    den_copy.start()

    load.wait()
    dft = dft_ref[...]

    def spectra(group, carry):
        for pair in range(TILE // 2):
            columns = []
            for which in range(2):
                row = group * TILE + pair * 2 + which
                gain = con_ref[pl.ds(row, 1), :]
                image = img_ref[row].astype(F32)
                columns.append(
                    jnp.concatenate([image[:, :CYCLES] * gain, image[:, CYCLES:] * gain], axis=0)
                )
            packed = jnp.concatenate(columns, axis=1).astype(BF16)
            out = jnp.dot(dft, packed, preferred_element_type=F32)
            out = out.astype(BF16).astype(F32)
            for which in range(2):
                row = group * TILE + pair * 2 + which
                lanes = out[:, which * CYCLES : (which + 1) * CYCLES]
                spec_re[pl.ds(row, ANGLES, stride=pitch), :] = lanes[:ANGLES]
                spec_im[pl.ds(row, ANGLES, stride=pitch), :] = lanes[ANGLES:]
        return carry

    groups = particles // TILE
    cuts = [0, groups // 4, groups // 2, groups * 3 // 4, groups]
    lax.fori_loop(cuts[0], cuts[1], spectra, 0)
    if chunk * chips > ANGLES:
        blank = jnp.zeros(((chunk * chips - ANGLES) * pitch, CYCLES), F32)
        spec_re[ANGLES * pitch :] = blank
        spec_im[ANGLES * pitch :] = blank

    den_copy.wait_recv()
    den_all[0] = den[...] + den_got[...]
    dens = []
    for e in range(1, chips):
        peer = lax.rem(chip + e, chips) * 2 + core
        copy = remote(den_all.at[0], den_all.at[e], e_send.at[e], e_recv.at[e], wide=peer)
        copy.start()
        dens.append(copy)
    for copy in first:
        copy.wait_recv()
    for step in range(STEPS):
        gath[me, step] = got[roster_ref[col, step]]
    outer = chips // 2
    place, inner = chip // 2, lax.rem(chip, 2)
    partner = (place * 2 + 1 - inner) * 2 + core
    second, third, fourth = [], [], []
    for e in range(1, outer):
        peer = (lax.rem(place + e, outer) * 2 + inner) * 2 + core
        copy = remote(gath.at[me], gath.at[me], b_send.at[e], b_recv.at[e], wide=peer)
        copy.start()
        second.append(copy)
    lax.fori_loop(cuts[1], cuts[2], spectra, 0)
    for e in range(outer):
        origin = (lax.rem(place + outer - e, outer) * 2 + inner) * 2 + core
        if e:
            second[e - 1].wait_recv()
        piece = gath.at[origin]
        copy = remote(piece, piece, y_send.at[e], y_recv.at[e], wide=partner)
        copy.start()
        third.append(copy)
        copy = remote(piece, piece, c_send.at[e], c_recv.at[e], wide=sibling)
        copy.start()
        fourth.append(copy)
    lax.fori_loop(cuts[2], cuts[3], spectra, 0)
    for e in range(outer):
        origin = (lax.rem(place + outer - e, outer) * 2 + 1 - inner) * 2 + core
        third[e].wait_recv()
        piece = gath.at[origin]
        copy = remote(piece, piece, c_send.at[outer + e], c_recv.at[outer + e], wide=sibling)
        copy.start()
        fourth.append(copy)
    lax.fori_loop(cuts[3], cuts[4], spectra, 0)

    lanes = OWN_MAX * CLS_GRP
    classes = narrow * CLS_GRP
    source, lane = iota((classes, lanes), 0), iota((classes, lanes), 1)
    spread = (source == col * CLS_GRP + lane % CLS_GRP).astype(F32).astype(BF16)
    owner_row = jnp.broadcast_to(owner_ref[...].astype(F32), (TILE, classes)).astype(BF16)
    owner_row = jnp.dot(owner_row, spread, preferred_element_type=F32)[0:1]
    shape = (wide * TILE, lanes)
    line, lane = iota(shape, 0), iota(shape, 1)
    held = (owner_row == (line // TILE).astype(F32)).astype(F32)
    before, after = iota((lanes, lanes), 0), iota((lanes, lanes), 1)
    counted = (before <= after) & (before // CLS_GRP == after // CLS_GRP)
    rank = jnp.dot(
        held.astype(BF16), counted.astype(F32).astype(BF16), preferred_element_type=F32
    )
    wanted = (rank - 1.0 == (line % OWN_MAX).astype(F32)).astype(F32)
    wanted = wanted * (lane // CLS_GRP == line // OWN_MAX % OWN_MAX).astype(F32)
    pick[...] = (held * wanted).astype(BF16)
    for copy in fourth:
        copy.wait_recv()

    rdft = rdft_ref[...]
    power = []
    for step in range(STEPS):
        for pair in range(block_classes // 2):
            columns = []
            for slot in (2 * pair, 2 * pair + 1):
                start = slot * 2 * pieces_each
                columns.append(
                    jnp.concatenate(
                        [gath[start + k, step] for k in range(2 * pieces_each)], axis=0
                    )
                )
            out = jnp.dot(rdft, jnp.concatenate(columns, axis=1), preferred_element_type=F32)
            out = out.astype(BF16).astype(F32)
            for which in range(2):
                c = step * block_classes + 2 * pair + which
                lanes = out[:, which * CYCLES : (which + 1) * CYCLES]
                real, imag = lanes[:ANGLES], lanes[ANGLES:]
                power.append(jnp.sum(real * real + imag * imag, axis=0, keepdims=True))
                plain = pl.ds(c, ANGLES, stride=row_pitch)
                turned = pl.ds(CLS_GRP + c, ANGLES, stride=row_pitch)
                rr_a[plain, :] = real
                rr_b[plain, :] = imag
                rr_a[turned, :] = -imag
                rr_b[turned, :] = real
    energy = lax.dot_general(
        jnp.concatenate(power, axis=0), squares, (((1,), (1,)), ((), ())),
        preferred_element_type=F32, precision=TOP,
    )

    def correlate(m, carry):
        rows = pl.ds(pl.multiple_of(m * row_pitch, 8), 2 * CLS_GRP)
        refs = jnp.concatenate([rr_a[rows, :], rr_b[rows, :]], axis=1).astype(BF16)
        lines = pl.ds(pl.multiple_of(m * pitch, 8), particles)
        image = jnp.concatenate([spec_re[lines, :], spec_im[lines, :]], axis=1).astype(BF16)
        ct[rows, :] = lax.dot_general(
            refs, image, (((1,), (1,)), ((), ())), preferred_element_type=F32
        )
        return carry

    lax.fori_loop(0, ANGLES, correlate, 0, unroll=8)

    angle = lax.broadcasted_iota(jnp.int32, (ANGLES, particles), 0)
    distance = jnp.abs(angle - rot_ref[...])
    distance = jnp.minimum(distance, ANGLES - distance).astype(F32)
    prior = -0.5 * jnp.square(distance / SIGMA_ROT)
    turn = turn_ref[...]
    chosen = jnp.zeros((ANGLES, particles), F32)
    best = None
    for step in range(STEPS):
        for pair in range(block_classes // 2):
            slots = (2 * pair, 2 * pair + 1)
            both = jnp.concatenate(
                [
                    jnp.concatenate(
                        [
                            ct[pl.ds(half + step * block_classes + s, ANGLES, stride=row_pitch), :]
                            for s in slots
                        ],
                        axis=1,
                    )
                    for half in (0, CLS_GRP)
                ],
                axis=0,
            )
            high, low = high_low(both)
            both = jnp.concatenate([high, low, high], axis=0).astype(BF16)
            turned = jnp.dot(turn, both, preferred_element_type=F32)
            for which, slot in enumerate(slots):
                c = step * block_classes + slot
                lanes = turned[:, which * particles : (which + 1) * particles]
                scores = (lanes - 0.5 * energy[c : c + 1]) / ANGLES + prior
                sc[c] = scores
                chosen = chosen + members[c : c + 1] * scores
                best = scores if best is None else jnp.maximum(best, scores)
    peak = jnp.max(best, axis=0, keepdims=True)
    total = jnp.zeros((ANGLES, particles), F32)
    for c in range(CLS_GRP):
        total = total + jnp.exp(sc[c] - peak)
    top[0:1] = peak
    top[1:2] = jnp.sum(total, axis=0, keepdims=True)
    tops = []
    for d in range(1, narrow):
        copy = remote(top, top_got.at[d], t_send.at[d], t_recv.at[d], narrow=lax.rem(col + d, narrow))
        copy.start()
        tops.append(copy)
    weight = jnp.exp(chosen - jnp.max(chosen, axis=0, keepdims=True))
    weight = weight / jnp.sum(weight, axis=0, keepdims=True)
    high, low = high_low(weight)
    weight = jnp.swapaxes(jnp.concatenate([high, high, low], axis=0), 0, 1).astype(BF16)
    coeff = jnp.dot(weight, tab_ref[...], preferred_element_type=F32)
    for place in range(chips):
        coeffs[place] = coeff[:, place * CYCLES : (place + 1) * CYCLES]
    picked = jnp.concatenate([members, jnp.zeros((8, particles), F32)], axis=0).astype(BF16)

    mine = pl.ds(pl.multiple_of(core * CYCLES, CYCLES), CYCLES)
    theirs = pl.ds(pl.multiple_of((1 - core) * CYCLES, CYCLES), CYCLES)
    flat = chunk * CLS_GRP
    padded = up(flat, 16)
    halves, parts = [], []

    def pass_on(e):
        place = lax.rem(chip + 1 + e, chips)
        rows = pl.ds(place * chunk, chunk)
        halves[e].wait_recv()
        both = num[rows, :, mine] + num_got[rows]
        if e == chips - 1:
            own[...] = both
            return
        both = both.reshape(flat, CYCLES)
        if padded > flat:
            both = jnp.concatenate([both, jnp.zeros((padded - flat, CYCLES), F32)], axis=0)
        part_out[e] = both.astype(BF16)
        copy = remote(
            part_out.at[e], part_got.at[e], p_send.at[e], p_recv.at[e], wide=place * 2 + core
        )
        copy.start()
        parts.append(copy)

    for e in range(chips):
        place = lax.rem(chip + 1 + e, chips)
        coeff = coeffs[place]
        for row in range(chunk):
            lines = pl.ds(pl.multiple_of((place * chunk + row) * pitch, 8), particles)
            x_real, x_imag = spec_re[lines, :], spec_im[lines, :]
            h_real = coeff[:, row : row + 1]
            h_imag = coeff[:, 64 + row : 65 + row]
            a_real = x_real * h_real - x_imag * h_imag
            a_imag = x_real * h_imag + x_imag * h_real
            aligned = jnp.concatenate([a_real, a_imag], axis=-1).astype(BF16)
            sums = jnp.dot(picked, aligned, preferred_element_type=F32)
            num[place * chunk + row] = sums[:CLS_GRP]
        rows = pl.ds(place * chunk, chunk)
        copy = remote(
            num.at[rows, :, theirs], num_got.at[rows], n_send.at[e], n_recv.at[e], wide=sibling
        )
        copy.start()
        halves.append(copy)
        if e:
            pass_on(e - 1)
    pass_on(chips - 1)

    peak, total = top[0:1], top[1:2]
    for d in range(1, narrow):
        tops[d - 1].wait_recv()
        other = top_got[d, 0:1]
        joined = jnp.maximum(peak, other)
        total = total * jnp.exp(peak - joined) + top_got[d, 1:2] * jnp.exp(other - joined)
        peak = joined
    ev_ref[...] = peak + jnp.log(total)
    for copy in dens:
        copy.wait_recv()
    scale = den_all[0]
    for e in range(1, chips):
        scale = scale + den_all[e]
    scale = 1.0 / (scale + TAU)
    for copy in parts:
        copy.wait_recv()
    summed = own[...].reshape(flat, CYCLES)
    for e in range(chips - 1):
        summed = summed + part_got[e].astype(F32)[:flat]
    summed = summed.reshape(chunk, CLS_GRP, CYCLES) * scale[None]
    quads = -(-chunk // OWN_MAX)
    blank = jnp.zeros((CLS_GRP, CYCLES), F32)
    for quad in range(quads):
        four = range(quad * OWN_MAX, (quad + 1) * OWN_MAX)
        four = jnp.concatenate([summed[r] if r < chunk else blank for r in four], axis=0)
        out = jnp.dot(pick[...], four.astype(BF16), preferred_element_type=F32)
        slot_out[:, quad] = out.astype(BF16).reshape(wide, TILE, CYCLES)
    slots = []
    for d in range(1, wide):
        peer = lax.rem(me + d, wide)
        copy = remote(slot_out.at[peer], har.at[core, chip], s_send.at[d], s_recv.at[d], wide=peer)
        copy.start()
        slots.append(copy)
    har[core, chip] = slot_out[me]
    for copy in slots:
        copy.wait_recv()
    length = chips * quads * TILE
    both = jnp.concatenate(
        [har[0].reshape(length, CYCLES), har[1].reshape(length, CYCLES)], axis=1
    )
    out = jnp.dot(back_ref[...], jnp.concatenate([both, both]), preferred_element_type=F32)
    size = OWN_MAX * ANGLES
    by_cos, by_sin = out[:size], out[size:]
    real = by_cos[:, :CYCLES] - by_sin[:, CYCLES:]
    imag = by_cos[:, CYCLES:] + by_sin[:, :CYCLES]
    for slot in range(OWN_MAX):
        span = slice(slot * ANGLES, (slot + 1) * ANGLES)
        new_ref[0, 0, slot, :, :CYCLES] = real[span].astype(BF16)
        new_ref[0, 0, slot, :, CYCLES:] = imag[span].astype(BF16)
    for copy in [den_copy] + first + second + third + fourth + halves + tops + dens + parts + slots:
        copy.wait_send()


def per_device(images, defocus, class_index, rotation_index, owner_map, roster, ref_store):
    wide = lax.axis_size("wide")
    narrow = lax.axis_size("narrow")
    chips = wide // 2
    chunk = -(-ANGLES // chips)
    quads = -(-chunk // OWN_MAX)
    particles = images.shape[0]
    cosines, sines = tables()

    block_classes = ref_store.shape[2]
    pieces_each = max(wide // (2 * block_classes), 1)
    rows = ANGLES // pieces_each
    height = up(rows, 16)

    dft = np.block([[cosines, sines], [-sines, cosines]]).astype(BF16)
    spaced = np.zeros((2 * ANGLES, 2, pieces_each, height), np.float32)
    spaced[..., :rows] = dft.astype(np.float32).reshape(2 * ANGLES, 2, pieces_each, rows)
    rdft = spaced.reshape(2 * ANGLES, -1).astype(BF16)
    turn = np.concatenate([cosines, -sines], axis=1)
    tab = np.zeros((chips, ANGLES, CYCLES), np.float32)
    back = np.zeros((2, OWN_MAX, ANGLES, chips, quads, OWN_MAX, OWN_MAX), np.float32)
    for m in range(ANGLES):
        place, row = divmod(m, chunk)
        tab[place, :, row] = cosines[:, m]
        tab[place, :, 64 + row] = sines[:, m]
        for slot in range(OWN_MAX):
            back[0, slot, :, place, row // OWN_MAX, row % OWN_MAX, slot] = cosines[m] / ANGLES
            back[1, slot, :, place, row // OWN_MAX, row % OWN_MAX, slot] = sines[m] / ANGLES
    back = back.reshape(2 * OWN_MAX * ANGLES, chips * quads * TILE)
    high, low = high_low(back)
    back = np.concatenate([high, low], axis=1).astype(BF16)
    high, low = high_low(turn)
    turn = np.concatenate([high, high, low], axis=1).astype(BF16)
    high, low = high_low(tab)
    tab = np.concatenate([high, low, high], axis=1).transpose(1, 0, 2).reshape(3 * ANGLES, -1)
    tab = tab.astype(BF16)

    vmem = pl.BlockSpec(memory_space=pltpu.VMEM)
    dma = pltpu.SemaphoreType.DMA
    flat = up(chunk * CLS_GRP, 16)
    new, evidence = pl.pallas_call(
        functools.partial(kernel, wide, narrow, chunk, pieces_each),
        out_shape=(
            jax.ShapeDtypeStruct((1, 1, OWN_MAX, ANGLES, 2 * CYCLES), BF16),
            jax.ShapeDtypeStruct((1, particles), F32),
        ),
        in_specs=[
            pl.BlockSpec(memory_space=pltpu.SMEM), vmem, pl.BlockSpec(memory_space=pl.ANY)
        ] + [vmem] * 9,
        out_specs=(vmem, vmem),
        scratch_shapes=[
            pltpu.VMEM((wide, height, CYCLES), BF16),
            pltpu.VMEM((particles, CYCLES), F32),
            pltpu.VMEM((particles, ANGLES, 2 * CYCLES), BF16),
            pltpu.VMEM((chunk * chips * (particles + 8), CYCLES), F32),
            pltpu.VMEM((chunk * chips * (particles + 8), CYCLES), F32),
            pltpu.VMEM((chips, particles, CYCLES), F32),
            pltpu.VMEM((wide, height, CYCLES), BF16),
            pltpu.VMEM((wide, STEPS, height, CYCLES), BF16),
            pltpu.VMEM((ANGLES * (2 * CLS_GRP + 8), CYCLES), F32),
            pltpu.VMEM((ANGLES * (2 * CLS_GRP + 8), CYCLES), F32),
            pltpu.VMEM((ANGLES * (2 * CLS_GRP + 8), particles), F32),
            pltpu.VMEM((CLS_GRP, ANGLES, particles), F32),
            pltpu.VMEM((chunk * chips, CLS_GRP, 2 * CYCLES), F32),
            pltpu.VMEM((chunk * chips, CLS_GRP, CYCLES), F32),
            pltpu.VMEM((CLS_GRP, CYCLES), F32),
            pltpu.VMEM((CLS_GRP, CYCLES), F32),
            pltpu.VMEM((chips, CLS_GRP, CYCLES), F32),
            pltpu.VMEM((8, particles), F32),
            pltpu.VMEM((narrow, 8, particles), F32),
            pltpu.VMEM((chips, flat, CYCLES), BF16),
            pltpu.VMEM((chips, flat, CYCLES), BF16),
            pltpu.VMEM((chunk, CLS_GRP, CYCLES), F32),
            pltpu.VMEM((wide * TILE, OWN_MAX * CLS_GRP), BF16),
            pltpu.VMEM((wide, quads, TILE, CYCLES), BF16),
            pltpu.VMEM((2, chips, quads, TILE, CYCLES), BF16),
            dma((1,)),
            dma((wide,)), dma((wide,)),
            dma((chips,)), dma((chips,)),
            dma((chips,)), dma((chips,)),
            dma((chips,)), dma((chips,)),
            dma((narrow,)), dma((narrow,)),
            dma((1,)), dma((1,)),
            dma((chips,)), dma((chips,)),
            dma((chips,)), dma((chips,)),
            dma((chips,)), dma((chips,)),
            dma((wide,)), dma((wide,)),
        ],
        compiler_params=pltpu.CompilerParams(
            collective_id=0, has_side_effects=True, vmem_limit_bytes=VMEM_LIMIT
        ),
        name="class_averages",
    )(
        roster, ref_store, images, defocus.reshape(1, particles),
        class_index.reshape(1, particles), rotation_index.reshape(1, particles),
        owner_map.reshape(1, narrow * CLS_GRP),
        jnp.asarray(dft), jnp.asarray(rdft), jnp.asarray(turn), jnp.asarray(tab), jnp.asarray(back),
    )
    return new, evidence.reshape(particles)


def solution(mesh):
    in_specs = (
        P("wide", None, None),
        P("wide"),
        P("wide"),
        P("wide"),
        P(),
        P(),
        P("wide", "narrow", None, None, None),
    )
    out_specs = (P("wide", "narrow", None, None, None), P("wide"))
    return jax.shard_map(
        per_device, mesh=mesh, in_specs=in_specs, out_specs=out_specs, check_vma=False
    )
```

```python
import functools
import math

import jax
import jax.numpy as jnp
import numpy as np
from jax import lax
from jax.experimental import pallas as pl
from jax.experimental.pallas import tpu as pltpu
from jax.sharding import PartitionSpec as P

CYCLES = 128
ANGLES = 72
STEPS = 3
OWN_MAX = 4
CLS_GRP = 24
SIGMA_ROT = 8
TAU = 1.0
CONTRAST = 0.1
TOP = lax.Precision.HIGHEST
MESH = pl.DeviceIdType.MESH
VMEM_LIMIT = 56 * 1024 * 1024
F32 = jnp.float32
BF16 = jnp.bfloat16
TILE = 16


def up(value, step):
    return -(-value // step) * step


def tables():
    counting = np.arange(ANGLES)
    phase = (counting[:, None] * counting[None, :] % ANGLES) * (2.0 * math.pi / ANGLES)
    return np.cos(phase).astype(np.float32), np.sin(phase).astype(np.float32)


def contrast(defocus_row):
    particles = defocus_row.shape[1]
    defocus = jnp.swapaxes(jnp.broadcast_to(defocus_row, (CYCLES, particles)), 0, 1)
    cycle = lax.broadcasted_iota(jnp.int32, (particles, CYCLES), 1).astype(F32)
    phase_angle = 8.0 * math.pi * defocus * jnp.square((cycle + 1.0) / CYCLES)
    return -jnp.sin(phase_angle) - CONTRAST * jnp.cos(phase_angle)


def high_low(value):
    high = value.astype(BF16).astype(value.dtype)
    return high, value - high


def fold(lane):
    total = jnp.zeros_like(lane)
    for edge in range(1, OWN_MAX):
        total = total + (lane >= edge * CLS_GRP).astype(jnp.int32)
    return total


def iota(shape, dimension):
    return lax.broadcasted_iota(jnp.int32, shape, dimension)


def remote(src, dst, send_sem, recv_sem, **target):
    return pltpu.make_async_remote_copy(
        src_ref=src,
        dst_ref=dst,
        send_sem=send_sem,
        recv_sem=recv_sem,
        device_id=target,
        device_id_type=MESH,
    )


def exact(a, b):
    return jnp.dot(a, b, preferred_element_type=F32, precision=TOP)


def kernel(
    wide, narrow, chunk, pieces_each,
    roster_ref, store_ref, img_hbm, defocus_ref, class_ref, rot_ref, owner_ref,
    dft_ref, rdft_ref, turn_ref, tab_ref, back_ref,
    new_ref, ev_ref,
    piece_ref, con_ref, img_ref, spec_re, spec_im, coeffs, got, gath, rr_a, rr_b, ct, sc, num, num_got, den, den_got, den_all, top, top_got,
    part_out, part_got, own, pick, slot_out, har,
    i_sem, a_send, a_recv, b_send, b_recv, y_send, y_recv, c_send, c_recv, t_send, t_recv, d_send, d_recv,
    e_send, e_recv, n_send, n_recv, p_send, p_recv, s_send, s_recv,
):
    me = lax.axis_index("wide")
    col = lax.axis_index("narrow")
    chips = wide // 2
    chip, core = me // 2, lax.rem(me, 2)
    sibling = chip * 2 + 1 - core
    particles = con_ref.shape[0]
    pitch = particles + 8
    row_pitch = 2 * CLS_GRP + 8
    block_classes = CLS_GRP // STEPS
    load = pltpu.make_async_copy(img_hbm, img_ref, i_sem.at[0])
    load.start()
    barrier = pltpu.get_barrier_semaphore()
    for d in range(1, wide):
        pl.semaphore_signal(
            barrier, inc=1, device_id={"wide": lax.rem(me + d, wide)}, device_id_type=MESH
        )
    for d in range(1, narrow):
        pl.semaphore_signal(
            barrier, inc=1, device_id={"narrow": lax.rem(col + d, narrow)}, device_id_type=MESH
        )
    rows = ANGLES // pieces_each
    height = piece_ref.shape[1]
    for part in range(pieces_each):
        row, angle = iota((height, ANGLES), 0), iota((height, ANGLES), 1)
        take = ((row + part * rows == angle) & (row < rows)).astype(F32).astype(BF16)
        for slot in range(block_classes):
            piece = jnp.dot(take, store_ref[0, 0, slot], preferred_element_type=F32).astype(BF16)
            for half in range(2):
                piece_ref[(slot * 2 + half) * pieces_each + part] = piece[
                    :, half * CYCLES : (half + 1) * CYCLES
                ]
    pl.semaphore_wait(barrier, wide + narrow - 2)

    first = []
    for d in range(1, wide):
        peer = lax.rem(me + d, wide)
        copy = remote(piece_ref.at[peer], got.at[me], a_send.at[d], a_recv.at[d], wide=peer)
        copy.start()
        first.append(copy)
    got[me] = piece_ref[me]

    con_ref[...] = contrast(defocus_ref[...])
    class_row = lax.broadcasted_iota(jnp.int32, (CLS_GRP, particles), 0) + col * CLS_GRP
    members = (class_row == class_ref[...]).astype(F32)
    squares = jnp.square(con_ref[...])
    den[...] = exact(members, squares)
    den_copy = remote(den, den_got, d_send.at[0], d_recv.at[0], wide=sibling)
    den_copy.start()

    load.wait()
    dft = dft_ref[...]

    def spectra(group, carry):
        for pair in range(TILE // 2):
            columns = []
            for which in range(2):
                row = group * TILE + pair * 2 + which
                gain = con_ref[pl.ds(row, 1), :]
                image = img_ref[row].astype(F32)
                columns.append(
                    jnp.concatenate([image[:, :CYCLES] * gain, image[:, CYCLES:] * gain], axis=0)
                )
            packed = jnp.concatenate(columns, axis=1).astype(BF16)
            out = jnp.dot(dft, packed, preferred_element_type=F32)
            out = out.astype(BF16).astype(F32)
            for which in range(2):
                row = group * TILE + pair * 2 + which
                lanes = out[:, which * CYCLES : (which + 1) * CYCLES]
                spec_re[pl.ds(row, ANGLES, stride=pitch), :] = lanes[:ANGLES]
                spec_im[pl.ds(row, ANGLES, stride=pitch), :] = lanes[ANGLES:]
        return carry

    groups = particles // TILE
    cuts = [0, groups // 4, groups // 2, groups * 3 // 4, groups]
    lax.fori_loop(cuts[0], cuts[1], spectra, 0)
    if chunk * chips > ANGLES:
        blank = jnp.zeros(((chunk * chips - ANGLES) * pitch, CYCLES), F32)
        spec_re[ANGLES * pitch :] = blank
        spec_im[ANGLES * pitch :] = blank

    den_copy.wait_recv()
    den_all[0] = den[...] + den_got[...]
    dens = []
    for e in range(1, chips):
        peer = lax.rem(chip + e, chips) * 2 + core
        copy = remote(den_all.at[0], den_all.at[e], e_send.at[e], e_recv.at[e], wide=peer)
        copy.start()
        dens.append(copy)
    for copy in first:
        copy.wait_recv()
    for step in range(STEPS):
        gath[me, step] = got[roster_ref[col, step]]
    outer = chips // 2
    place, inner = chip // 2, lax.rem(chip, 2)
    partner = (place * 2 + 1 - inner) * 2 + core
    second, third, fourth = [], [], []
    for e in range(1, outer):
        peer = (lax.rem(place + e, outer) * 2 + inner) * 2 + core
        copy = remote(gath.at[me], gath.at[me], b_send.at[e], b_recv.at[e], wide=peer)
        copy.start()
        second.append(copy)
    lax.fori_loop(cuts[1], cuts[2], spectra, 0)
    for e in range(outer):
        origin = (lax.rem(place + outer - e, outer) * 2 + inner) * 2 + core
        if e:
            second[e - 1].wait_recv()
        piece = gath.at[origin]
        copy = remote(piece, piece, y_send.at[e], y_recv.at[e], wide=partner)
        copy.start()
        third.append(copy)
        copy = remote(piece, piece, c_send.at[e], c_recv.at[e], wide=sibling)
        copy.start()
        fourth.append(copy)
    lax.fori_loop(cuts[2], cuts[3], spectra, 0)
    for e in range(outer):
        origin = (lax.rem(place + outer - e, outer) * 2 + 1 - inner) * 2 + core
        third[e].wait_recv()
        piece = gath.at[origin]
        copy = remote(piece, piece, c_send.at[outer + e], c_recv.at[outer + e], wide=sibling)
        copy.start()
        fourth.append(copy)
    lax.fori_loop(cuts[3], cuts[4], spectra, 0)

    lanes = OWN_MAX * CLS_GRP
    classes = narrow * CLS_GRP
    source, lane = iota((classes, lanes), 0), iota((classes, lanes), 1)
    spread = (source == col * CLS_GRP + lane - fold(lane) * CLS_GRP).astype(F32).astype(BF16)
    owner_row = jnp.broadcast_to(owner_ref[...].astype(F32), (TILE, classes)).astype(BF16)
    owner_row = jnp.dot(owner_row, spread, preferred_element_type=F32)[0:1]
    shape = (wide * TILE, lanes)
    line, lane = iota(shape, 0), iota(shape, 1)
    held = (owner_row == (line >> 4).astype(F32)).astype(F32)
    before, after = iota((lanes, lanes), 0), iota((lanes, lanes), 1)
    counted = (before <= after) & (fold(before) == fold(after))
    rank = jnp.dot(
        held.astype(BF16), counted.astype(F32).astype(BF16), preferred_element_type=F32
    )
    wanted = (rank - 1.0 == (line & 3).astype(F32)).astype(F32)
    wanted = wanted * (fold(lane) == ((line >> 2) & 3)).astype(F32)
    pick[...] = (held * wanted).astype(BF16)
    for copy in fourth:
        copy.wait_recv()

    rdft = rdft_ref[...]
    power = []
    for step in range(STEPS):
        for pair in range(block_classes // 2):
            columns = []
            for slot in (2 * pair, 2 * pair + 1):
                start = slot * 2 * pieces_each
                columns.append(
                    jnp.concatenate(
                        [gath[start + k, step] for k in range(2 * pieces_each)], axis=0
                    )
                )
            out = jnp.dot(rdft, jnp.concatenate(columns, axis=1), preferred_element_type=F32)
            out = out.astype(BF16).astype(F32)
            for which in range(2):
                c = step * block_classes + 2 * pair + which
                lanes = out[:, which * CYCLES : (which + 1) * CYCLES]
                real, imag = lanes[:ANGLES], lanes[ANGLES:]
                power.append(jnp.sum(real * real + imag * imag, axis=0, keepdims=True))
                plain = pl.ds(c, ANGLES, stride=row_pitch)
                turned = pl.ds(CLS_GRP + c, ANGLES, stride=row_pitch)
                rr_a[plain, :] = real
                rr_b[plain, :] = imag
                rr_a[turned, :] = -imag
                rr_b[turned, :] = real
    energy = lax.dot_general(
        jnp.concatenate(power, axis=0), squares, (((1,), (1,)), ((), ())),
        preferred_element_type=F32, precision=TOP,
    )

    def correlate(m, carry):
        rows = pl.ds(pl.multiple_of(m * row_pitch, 8), 2 * CLS_GRP)
        refs = jnp.concatenate([rr_a[rows, :], rr_b[rows, :]], axis=1).astype(BF16)
        lines = pl.ds(pl.multiple_of(m * pitch, 8), particles)
        image = jnp.concatenate([spec_re[lines, :], spec_im[lines, :]], axis=1).astype(BF16)
        ct[rows, :] = lax.dot_general(
            refs, image, (((1,), (1,)), ((), ())), preferred_element_type=F32
        )
        return carry

    lax.fori_loop(0, ANGLES, correlate, 0, unroll=8)

    angle = lax.broadcasted_iota(jnp.int32, (ANGLES, particles), 0)
    distance = jnp.abs(angle - rot_ref[...])
    distance = jnp.minimum(distance, ANGLES - distance).astype(F32)
    prior = -0.5 * jnp.square(distance / SIGMA_ROT)
    turn = turn_ref[...]
    chosen = jnp.zeros((ANGLES, particles), F32)
    best = None
    for step in range(STEPS):
        for pair in range(block_classes // 2):
            slots = (2 * pair, 2 * pair + 1)
            both = jnp.concatenate(
                [
                    jnp.concatenate(
                        [
                            ct[pl.ds(half + step * block_classes + s, ANGLES, stride=row_pitch), :]
                            for s in slots
                        ],
                        axis=1,
                    )
                    for half in (0, CLS_GRP)
                ],
                axis=0,
            )
            high, low = high_low(both)
            both = jnp.concatenate([high, low, high], axis=0).astype(BF16)
            turned = jnp.dot(turn, both, preferred_element_type=F32)
            for which, slot in enumerate(slots):
                c = step * block_classes + slot
                lanes = turned[:, which * particles : (which + 1) * particles]
                scores = (lanes - 0.5 * energy[c : c + 1]) / ANGLES + prior
                sc[c] = scores
                chosen = chosen + members[c : c + 1] * scores
                best = scores if best is None else jnp.maximum(best, scores)
    peak = jnp.max(best, axis=0, keepdims=True)
    total = jnp.zeros((ANGLES, particles), F32)
    for c in range(CLS_GRP):
        total = total + jnp.exp(sc[c] - peak)
    top[0:1] = peak
    top[1:2] = jnp.sum(total, axis=0, keepdims=True)
    tops = []
    for d in range(1, narrow):
        copy = remote(top, top_got.at[d], t_send.at[d], t_recv.at[d], narrow=lax.rem(col + d, narrow))
        copy.start()
        tops.append(copy)
    weight = jnp.exp(chosen - jnp.max(chosen, axis=0, keepdims=True))
    weight = weight / jnp.sum(weight, axis=0, keepdims=True)
    high, low = high_low(weight)
    weight = jnp.swapaxes(jnp.concatenate([high, high, low], axis=0), 0, 1).astype(BF16)
    coeff = jnp.dot(weight, tab_ref[...], preferred_element_type=F32)
    for place in range(chips):
        coeffs[place] = coeff[:, place * CYCLES : (place + 1) * CYCLES]
    picked = jnp.concatenate([members, jnp.zeros((8, particles), F32)], axis=0).astype(BF16)

    mine = pl.ds(pl.multiple_of(core * CYCLES, CYCLES), CYCLES)
    theirs = pl.ds(pl.multiple_of((1 - core) * CYCLES, CYCLES), CYCLES)
    flat = chunk * CLS_GRP
    padded = up(flat, 16)
    halves, crossing, parts = [], [], []

    level = chip // 2

    def chunk_at(i):
        side = inner if i % 2 else 1 - inner
        return lax.rem(level + 1 + i // 2, outer) * 2 + side

    def pass_on(i):
        e, place = i // 2, chunk_at(i)
        rows = pl.ds(place * chunk, chunk)
        halves[i].wait_recv()
        both = (num[rows, :, mine] + num_got[rows]).reshape(flat, CYCLES)
        if padded > flat:
            both = jnp.concatenate([both, jnp.zeros((padded - flat, CYCLES), F32)], axis=0)
        if i % 2:
            crossing[e].wait_recv()
            both = both + part_got[e].astype(F32)
            if e == outer - 1:
                own[...] = both
                return
            slot, peer = outer + e, place * 2 + core
        else:
            slot, peer = e, partner
        part_out[slot] = both.astype(BF16)
        copy = remote(
            part_out.at[slot], part_got.at[slot], p_send.at[slot], p_recv.at[slot], wide=peer
        )
        copy.start()
        if i % 2:
            parts.append(copy)
        else:
            crossing.append(copy)

    for i in range(chips):
        place = chunk_at(i)
        coeff = coeffs[place]
        for row in range(chunk):
            lines = pl.ds(pl.multiple_of((place * chunk + row) * pitch, 8), particles)
            x_real, x_imag = spec_re[lines, :], spec_im[lines, :]
            h_real = coeff[:, row : row + 1]
            h_imag = coeff[:, 64 + row : 65 + row]
            a_real = x_real * h_real - x_imag * h_imag
            a_imag = x_real * h_imag + x_imag * h_real
            aligned = jnp.concatenate([a_real, a_imag], axis=-1).astype(BF16)
            sums = jnp.dot(picked, aligned, preferred_element_type=F32)
            num[place * chunk + row] = sums[:CLS_GRP]
        rows = pl.ds(place * chunk, chunk)
        copy = remote(
            num.at[rows, :, theirs], num_got.at[rows], n_send.at[i], n_recv.at[i], wide=sibling
        )
        copy.start()
        halves.append(copy)
        if i % 2:
            pass_on(i - 1)
            if i > 2:
                pass_on(i - 2)
    pass_on(chips - 1)

    peak, total = top[0:1], top[1:2]
    for d in range(1, narrow):
        tops[d - 1].wait_recv()
        other = top_got[d, 0:1]
        joined = jnp.maximum(peak, other)
        total = total * jnp.exp(peak - joined) + top_got[d, 1:2] * jnp.exp(other - joined)
        peak = joined
    ev_ref[...] = peak + jnp.log(total)
    for copy in dens:
        copy.wait_recv()
    scale = den_all[0]
    for e in range(1, chips):
        scale = scale + den_all[e]
    scale = 1.0 / (scale + TAU)
    for copy in parts:
        copy.wait_recv()
    summed = own[...]
    for e in range(outer - 1):
        summed = summed + part_got[outer + e].astype(F32)
    summed = summed[:flat].reshape(chunk, CLS_GRP, CYCLES) * scale[None]
    quads = -(-chunk // OWN_MAX)
    blank = jnp.zeros((CLS_GRP, CYCLES), F32)
    for quad in range(quads):
        four = range(quad * OWN_MAX, (quad + 1) * OWN_MAX)
        four = jnp.concatenate([summed[r] if r < chunk else blank for r in four], axis=0)
        out = jnp.dot(pick[...], four.astype(BF16), preferred_element_type=F32)
        slot_out[:, quad] = out.astype(BF16).reshape(wide, TILE, CYCLES)
    slots = []
    for d in range(1, wide):
        peer = lax.rem(me + d, wide)
        copy = remote(slot_out.at[peer], har.at[core, chip], s_send.at[d], s_recv.at[d], wide=peer)
        copy.start()
        slots.append(copy)
    har[core, chip] = slot_out[me]
    for copy in slots:
        copy.wait_recv()
    length = chips * quads * TILE
    both = jnp.concatenate(
        [har[0].reshape(length, CYCLES), har[1].reshape(length, CYCLES)], axis=1
    )
    out = jnp.dot(back_ref[...], jnp.concatenate([both, both]), preferred_element_type=F32)
    size = OWN_MAX * ANGLES
    by_cos, by_sin = out[:size], out[size:]
    real = by_cos[:, :CYCLES] - by_sin[:, CYCLES:]
    imag = by_cos[:, CYCLES:] + by_sin[:, :CYCLES]
    for slot in range(OWN_MAX):
        span = slice(slot * ANGLES, (slot + 1) * ANGLES)
        new_ref[0, 0, slot, :, :CYCLES] = real[span].astype(BF16)
        new_ref[0, 0, slot, :, CYCLES:] = imag[span].astype(BF16)
    for copy in [den_copy] + first + second + third + fourth + halves + tops + dens + crossing + parts + slots:
        copy.wait_send()


def per_device(images, defocus, class_index, rotation_index, owner_map, roster, ref_store):
    wide = lax.axis_size("wide")
    narrow = lax.axis_size("narrow")
    chips = wide // 2
    chunk = -(-ANGLES // chips)
    quads = -(-chunk // OWN_MAX)
    particles = images.shape[0]
    cosines, sines = tables()

    block_classes = ref_store.shape[2]
    pieces_each = max(wide // (2 * block_classes), 1)
    rows = ANGLES // pieces_each
    height = up(rows, 16)

    dft = np.block([[cosines, sines], [-sines, cosines]]).astype(BF16)
    spaced = np.zeros((2 * ANGLES, 2, pieces_each, height), np.float32)
    spaced[..., :rows] = dft.astype(np.float32).reshape(2 * ANGLES, 2, pieces_each, rows)
    rdft = spaced.reshape(2 * ANGLES, -1).astype(BF16)
    turn = np.concatenate([cosines, -sines], axis=1)
    tab = np.zeros((chips, ANGLES, CYCLES), np.float32)
    back = np.zeros((2, OWN_MAX, ANGLES, chips, quads, OWN_MAX, OWN_MAX), np.float32)
    for m in range(ANGLES):
        place, row = divmod(m, chunk)
        tab[place, :, row] = cosines[:, m]
        tab[place, :, 64 + row] = sines[:, m]
        for slot in range(OWN_MAX):
            back[0, slot, :, place, row // OWN_MAX, row % OWN_MAX, slot] = cosines[m] / ANGLES
            back[1, slot, :, place, row // OWN_MAX, row % OWN_MAX, slot] = sines[m] / ANGLES
    back = back.reshape(2 * OWN_MAX * ANGLES, chips * quads * TILE)
    high, low = high_low(back)
    back = np.concatenate([high, low], axis=1).astype(BF16)
    high, low = high_low(turn)
    turn = np.concatenate([high, high, low], axis=1).astype(BF16)
    high, low = high_low(tab)
    tab = np.concatenate([high, low, high], axis=1).transpose(1, 0, 2).reshape(3 * ANGLES, -1)
    tab = tab.astype(BF16)

    vmem = pl.BlockSpec(memory_space=pltpu.VMEM)
    dma = pltpu.SemaphoreType.DMA
    flat = up(chunk * CLS_GRP, 16)
    new, evidence = pl.pallas_call(
        functools.partial(kernel, wide, narrow, chunk, pieces_each),
        out_shape=(
            jax.ShapeDtypeStruct((1, 1, OWN_MAX, ANGLES, 2 * CYCLES), BF16),
            jax.ShapeDtypeStruct((1, particles), F32),
        ),
        in_specs=[
            pl.BlockSpec(memory_space=pltpu.SMEM), vmem, pl.BlockSpec(memory_space=pl.ANY)
        ] + [vmem] * 9,
        out_specs=(vmem, vmem),
        scratch_shapes=[
            pltpu.VMEM((wide, height, CYCLES), BF16),
            pltpu.VMEM((particles, CYCLES), F32),
            pltpu.VMEM((particles, ANGLES, 2 * CYCLES), BF16),
            pltpu.VMEM((chunk * chips * (particles + 8), CYCLES), F32),
            pltpu.VMEM((chunk * chips * (particles + 8), CYCLES), F32),
            pltpu.VMEM((chips, particles, CYCLES), F32),
            pltpu.VMEM((wide, height, CYCLES), BF16),
            pltpu.VMEM((wide, STEPS, height, CYCLES), BF16),
            pltpu.VMEM((ANGLES * (2 * CLS_GRP + 8), CYCLES), F32),
            pltpu.VMEM((ANGLES * (2 * CLS_GRP + 8), CYCLES), F32),
            pltpu.VMEM((ANGLES * (2 * CLS_GRP + 8), particles), F32),
            pltpu.VMEM((CLS_GRP, ANGLES, particles), F32),
            pltpu.VMEM((chunk * chips, CLS_GRP, 2 * CYCLES), F32),
            pltpu.VMEM((chunk * chips, CLS_GRP, CYCLES), F32),
            pltpu.VMEM((CLS_GRP, CYCLES), F32),
            pltpu.VMEM((CLS_GRP, CYCLES), F32),
            pltpu.VMEM((chips, CLS_GRP, CYCLES), F32),
            pltpu.VMEM((8, particles), F32),
            pltpu.VMEM((narrow, 8, particles), F32),
            pltpu.VMEM((chips, flat, CYCLES), BF16),
            pltpu.VMEM((chips, flat, CYCLES), BF16),
            pltpu.VMEM((flat, CYCLES), F32),
            pltpu.VMEM((wide * TILE, OWN_MAX * CLS_GRP), BF16),
            pltpu.VMEM((wide, quads, TILE, CYCLES), BF16),
            pltpu.VMEM((2, chips, quads, TILE, CYCLES), BF16),
            dma((1,)),
            dma((wide,)), dma((wide,)),
            dma((chips,)), dma((chips,)),
            dma((chips,)), dma((chips,)),
            dma((chips,)), dma((chips,)),
            dma((narrow,)), dma((narrow,)),
            dma((1,)), dma((1,)),
            dma((chips,)), dma((chips,)),
            dma((chips,)), dma((chips,)),
            dma((chips,)), dma((chips,)),
            dma((wide,)), dma((wide,)),
        ],
        compiler_params=pltpu.CompilerParams(
            collective_id=0, has_side_effects=True, vmem_limit_bytes=VMEM_LIMIT
        ),
        name="class_averages",
    )(
        roster, ref_store, images, defocus.reshape(1, particles),
        class_index.reshape(1, particles), rotation_index.reshape(1, particles),
        owner_map.reshape(1, narrow * CLS_GRP),
        jnp.asarray(dft), jnp.asarray(rdft), jnp.asarray(turn), jnp.asarray(tab), jnp.asarray(back),
    )
    return new, evidence.reshape(particles)


def solution(mesh):
    in_specs = (
        P("wide", None, None),
        P("wide"),
        P("wide"),
        P("wide"),
        P(),
        P(),
        P("wide", "narrow", None, None, None),
    )
    out_specs = (P("wide", "narrow", None, None, None), P("wide"))
    return jax.shard_map(
        per_device, mesh=mesh, in_specs=in_specs, out_specs=out_specs, check_vma=False
    )
```

```python
import functools
import math

import jax
import jax.numpy as jnp
import numpy as np
from jax import lax
from jax.experimental import pallas as pl
from jax.experimental.pallas import tpu as pltpu
from jax.sharding import PartitionSpec as P

CYCLES = 128
ANGLES = 72
STEPS = 3
OWN_MAX = 4
CLS_GRP = 24
SIGMA_ROT = 8
TAU = 1.0
CONTRAST = 0.1
TOP = lax.Precision.HIGHEST
MESH = pl.DeviceIdType.MESH
VMEM_LIMIT = 56 * 1024 * 1024
F32 = jnp.float32
BF16 = jnp.bfloat16
TILE = 16


def up(value, step):
    return -(-value // step) * step


def tables():
    counting = np.arange(ANGLES)
    phase = (counting[:, None] * counting[None, :] % ANGLES) * (2.0 * math.pi / ANGLES)
    return np.cos(phase).astype(np.float32), np.sin(phase).astype(np.float32)


def contrast(defocus_row):
    particles = defocus_row.shape[1]
    defocus = jnp.swapaxes(jnp.broadcast_to(defocus_row, (CYCLES, particles)), 0, 1)
    cycle = lax.broadcasted_iota(jnp.int32, (particles, CYCLES), 1).astype(F32)
    phase_angle = 8.0 * math.pi * defocus * jnp.square((cycle + 1.0) / CYCLES)
    return -jnp.sin(phase_angle) - CONTRAST * jnp.cos(phase_angle)


def high_low(value):
    high = value.astype(BF16).astype(value.dtype)
    return high, value - high


def fold(lane):
    total = jnp.zeros_like(lane)
    for edge in range(1, OWN_MAX):
        total = total + (lane >= edge * CLS_GRP).astype(jnp.int32)
    return total


def iota(shape, dimension):
    return lax.broadcasted_iota(jnp.int32, shape, dimension)


def remote(src, dst, send_sem, recv_sem, **target):
    return pltpu.make_async_remote_copy(
        src_ref=src,
        dst_ref=dst,
        send_sem=send_sem,
        recv_sem=recv_sem,
        device_id=target,
        device_id_type=MESH,
    )


def exact(a, b):
    return jnp.dot(a, b, preferred_element_type=F32, precision=TOP)


def kernel(
    wide, narrow, chunk, pieces_each,
    roster_ref, store_ref, img_hbm, defocus_ref, class_ref, rot_ref, owner_ref,
    dft_ref, rdft_ref, turn_ref, tab_ref, back_ref,
    new_ref, ev_ref,
    piece_ref, con_ref, img_ref, spec_re, spec_im, coeffs, got, gath, rr_a, rr_b, ct, sc, num, num_got, den, den_got, den_all, top, top_got,
    part_out, part_got, own, pick, slot_out, har,
    i_sem, a_send, a_recv, b_send, b_recv, y_send, y_recv, c_send, c_recv, t_send, t_recv, d_send, d_recv,
    e_send, e_recv, n_send, n_recv, p_send, p_recv, s_send, s_recv,
):
    me = lax.axis_index("wide")
    col = lax.axis_index("narrow")
    chips = wide // 2
    chip, core = me // 2, lax.rem(me, 2)
    sibling = chip * 2 + 1 - core
    particles = con_ref.shape[0]
    pitch = particles + 8
    row_pitch = 2 * CLS_GRP + 8
    block_classes = CLS_GRP // STEPS
    load = pltpu.make_async_copy(img_hbm, img_ref, i_sem.at[0])
    load.start()
    barrier = pltpu.get_barrier_semaphore()
    for d in range(1, wide):
        pl.semaphore_signal(
            barrier, inc=1, device_id={"wide": lax.rem(me + d, wide)}, device_id_type=MESH
        )
    for d in range(1, narrow):
        pl.semaphore_signal(
            barrier, inc=1, device_id={"narrow": lax.rem(col + d, narrow)}, device_id_type=MESH
        )
    rows = ANGLES // pieces_each
    height = piece_ref.shape[1]
    for part in range(pieces_each):
        row, angle = iota((height, ANGLES), 0), iota((height, ANGLES), 1)
        take = ((row + part * rows == angle) & (row < rows)).astype(F32).astype(BF16)
        for slot in range(block_classes):
            piece = jnp.dot(take, store_ref[0, 0, slot], preferred_element_type=F32).astype(BF16)
            for half in range(2):
                piece_ref[(slot * 2 + half) * pieces_each + part] = piece[
                    :, half * CYCLES : (half + 1) * CYCLES
                ]
    pl.semaphore_wait(barrier, wide + narrow - 2)

    first = []
    for d in range(1, wide):
        peer = lax.rem(me + d, wide)
        copy = remote(piece_ref.at[peer], got.at[me], a_send.at[d], a_recv.at[d], wide=peer)
        copy.start()
        first.append(copy)
    got[me] = piece_ref[me]

    con_ref[...] = contrast(defocus_ref[...])
    class_row = lax.broadcasted_iota(jnp.int32, (CLS_GRP, particles), 0) + col * CLS_GRP
    members = (class_row == class_ref[...]).astype(F32)
    squares = jnp.square(con_ref[...])
    den[...] = exact(members, squares)
    den_copy = remote(den, den_got, d_send.at[0], d_recv.at[0], wide=sibling)
    den_copy.start()

    load.wait()
    dft = dft_ref[...]

    def spectra(group, carry):
        for pair in range(TILE // 2):
            columns = []
            for which in range(2):
                row = group * TILE + pair * 2 + which
                gain = con_ref[pl.ds(row, 1), :]
                image = img_ref[row].astype(F32)
                columns.append(
                    jnp.concatenate([image[:, :CYCLES] * gain, image[:, CYCLES:] * gain], axis=0)
                )
            packed = jnp.concatenate(columns, axis=1).astype(BF16)
            out = jnp.dot(dft, packed, preferred_element_type=F32)
            out = out.astype(BF16).astype(F32)
            for which in range(2):
                row = group * TILE + pair * 2 + which
                lanes = out[:, which * CYCLES : (which + 1) * CYCLES]
                spec_re[pl.ds(row, ANGLES, stride=pitch), :] = lanes[:ANGLES]
                spec_im[pl.ds(row, ANGLES, stride=pitch), :] = lanes[ANGLES:]
        return carry

    groups = particles // TILE
    cuts = [0, groups // 2, groups * 5 // 8, groups * 3 // 4, groups]
    lax.fori_loop(cuts[0], cuts[1], spectra, 0)
    if chunk * chips > ANGLES:
        blank = jnp.zeros(((chunk * chips - ANGLES) * pitch, CYCLES), F32)
        spec_re[ANGLES * pitch :] = blank
        spec_im[ANGLES * pitch :] = blank

    den_copy.wait_recv()
    den_all[0] = den[...] + den_got[...]
    dens = []
    for e in range(1, chips):
        peer = lax.rem(chip + e, chips) * 2 + core
        copy = remote(den_all.at[0], den_all.at[e], e_send.at[e], e_recv.at[e], wide=peer)
        copy.start()
        dens.append(copy)
    lanes = OWN_MAX * CLS_GRP
    classes = narrow * CLS_GRP
    source, lane = iota((classes, lanes), 0), iota((classes, lanes), 1)
    spread = (source == col * CLS_GRP + lane - fold(lane) * CLS_GRP).astype(F32).astype(BF16)
    owner_row = jnp.broadcast_to(owner_ref[...].astype(F32), (TILE, classes)).astype(BF16)
    owner_row = jnp.dot(owner_row, spread, preferred_element_type=F32)[0:1]
    shape = (wide * TILE, lanes)
    line, lane = iota(shape, 0), iota(shape, 1)
    held = (owner_row == (line >> 4).astype(F32)).astype(F32)
    before, after = iota((lanes, lanes), 0), iota((lanes, lanes), 1)
    counted = (before <= after) & (fold(before) == fold(after))
    rank = jnp.dot(
        held.astype(BF16), counted.astype(F32).astype(BF16), preferred_element_type=F32
    )
    wanted = (rank - 1.0 == (line & 3).astype(F32)).astype(F32)
    wanted = wanted * (fold(lane) == ((line >> 2) & 3)).astype(F32)
    pick[...] = (held * wanted).astype(BF16)
    for copy in first:
        copy.wait_recv()
    for step in range(STEPS):
        gath[me, step] = got[roster_ref[col, step]]
    outer = chips // 2
    place, inner = chip // 2, lax.rem(chip, 2)
    partner = (place * 2 + 1 - inner) * 2 + core
    second, third, fourth = [], [], []
    for e in range(1, outer):
        peer = (lax.rem(place + e, outer) * 2 + inner) * 2 + core
        copy = remote(gath.at[me], gath.at[me], b_send.at[e], b_recv.at[e], wide=peer)
        copy.start()
        second.append(copy)
    for e in range(outer):
        if e == 1:
            lax.fori_loop(cuts[1], cuts[2], spectra, 0)
        origin = (lax.rem(place + outer - e, outer) * 2 + inner) * 2 + core
        if e:
            second[e - 1].wait_recv()
        piece = gath.at[origin]
        copy = remote(piece, piece, y_send.at[e], y_recv.at[e], wide=partner)
        copy.start()
        third.append(copy)
        copy = remote(piece, piece, c_send.at[e], c_recv.at[e], wide=sibling)
        copy.start()
        fourth.append(copy)
    lax.fori_loop(cuts[2], cuts[3], spectra, 0)
    for e in range(outer):
        origin = (lax.rem(place + outer - e, outer) * 2 + 1 - inner) * 2 + core
        third[e].wait_recv()
        piece = gath.at[origin]
        copy = remote(piece, piece, c_send.at[outer + e], c_recv.at[outer + e], wide=sibling)
        copy.start()
        fourth.append(copy)
    lax.fori_loop(cuts[3], cuts[4], spectra, 0)

    for copy in fourth:
        copy.wait_recv()

    rdft = rdft_ref[...]
    power = []
    for step in range(STEPS):
        for pair in range(block_classes // 2):
            columns = []
            for slot in (2 * pair, 2 * pair + 1):
                start = slot * 2 * pieces_each
                columns.append(
                    jnp.concatenate(
                        [gath[start + k, step] for k in range(2 * pieces_each)], axis=0
                    )
                )
            out = jnp.dot(rdft, jnp.concatenate(columns, axis=1), preferred_element_type=F32)
            out = out.astype(BF16).astype(F32)
            for which in range(2):
                c = step * block_classes + 2 * pair + which
                lanes = out[:, which * CYCLES : (which + 1) * CYCLES]
                real, imag = lanes[:ANGLES], lanes[ANGLES:]
                power.append(jnp.sum(real * real + imag * imag, axis=0, keepdims=True))
                plain = pl.ds(c, ANGLES, stride=row_pitch)
                turned = pl.ds(CLS_GRP + c, ANGLES, stride=row_pitch)
                rr_a[plain, :] = real
                rr_b[plain, :] = imag
                rr_a[turned, :] = -imag
                rr_b[turned, :] = real
    energy = lax.dot_general(
        jnp.concatenate(power, axis=0), squares, (((1,), (1,)), ((), ())),
        preferred_element_type=F32, precision=TOP,
    )

    def correlate(m, carry):
        rows = pl.ds(pl.multiple_of(m * row_pitch, 8), 2 * CLS_GRP)
        refs = jnp.concatenate([rr_a[rows, :], rr_b[rows, :]], axis=1).astype(BF16)
        lines = pl.ds(pl.multiple_of(m * pitch, 8), particles)
        image = jnp.concatenate([spec_re[lines, :], spec_im[lines, :]], axis=1).astype(BF16)
        ct[rows, :] = lax.dot_general(
            refs, image, (((1,), (1,)), ((), ())), preferred_element_type=F32
        )
        return carry

    lax.fori_loop(0, ANGLES, correlate, 0, unroll=8)

    angle = lax.broadcasted_iota(jnp.int32, (ANGLES, particles), 0)
    distance = jnp.abs(angle - rot_ref[...])
    distance = jnp.minimum(distance, ANGLES - distance).astype(F32)
    prior = -0.5 * jnp.square(distance / SIGMA_ROT)
    turn = turn_ref[...]
    chosen = jnp.zeros((ANGLES, particles), F32)
    best = None
    for step in range(STEPS):
        for pair in range(block_classes // 2):
            slots = (2 * pair, 2 * pair + 1)
            both = jnp.concatenate(
                [
                    jnp.concatenate(
                        [
                            ct[pl.ds(half + step * block_classes + s, ANGLES, stride=row_pitch), :]
                            for s in slots
                        ],
                        axis=1,
                    )
                    for half in (0, CLS_GRP)
                ],
                axis=0,
            )
            high, low = high_low(both)
            both = jnp.concatenate([high, low, high], axis=0).astype(BF16)
            turned = jnp.dot(turn, both, preferred_element_type=F32)
            for which, slot in enumerate(slots):
                c = step * block_classes + slot
                lanes = turned[:, which * particles : (which + 1) * particles]
                scores = (lanes - 0.5 * energy[c : c + 1]) / ANGLES + prior
                sc[c] = scores
                chosen = chosen + members[c : c + 1] * scores
                best = scores if best is None else jnp.maximum(best, scores)
    peak = jnp.max(best, axis=0, keepdims=True)
    total = jnp.zeros((ANGLES, particles), F32)
    for c in range(CLS_GRP):
        total = total + jnp.exp(sc[c] - peak)
    top[0:1] = peak
    top[1:2] = jnp.sum(total, axis=0, keepdims=True)
    tops = []
    for d in range(1, narrow):
        copy = remote(top, top_got.at[d], t_send.at[d], t_recv.at[d], narrow=lax.rem(col + d, narrow))
        copy.start()
        tops.append(copy)
    weight = jnp.exp(chosen - jnp.max(chosen, axis=0, keepdims=True))
    weight = weight / jnp.sum(weight, axis=0, keepdims=True)
    high, low = high_low(weight)
    weight = jnp.swapaxes(jnp.concatenate([high, high, low], axis=0), 0, 1).astype(BF16)
    coeff = jnp.dot(weight, tab_ref[...], preferred_element_type=F32)
    for place in range(chips):
        coeffs[place] = coeff[:, place * CYCLES : (place + 1) * CYCLES]
    picked = jnp.concatenate([members, jnp.zeros((8, particles), F32)], axis=0).astype(BF16)

    mine = pl.ds(pl.multiple_of(core * CYCLES, CYCLES), CYCLES)
    theirs = pl.ds(pl.multiple_of((1 - core) * CYCLES, CYCLES), CYCLES)
    flat = chunk * CLS_GRP
    padded = up(flat, 16)
    halves, crossing, parts = [], [], []

    level = chip // 2

    def chunk_at(i):
        side = inner if i % 2 else 1 - inner
        return lax.rem(level + 1 + i // 2, outer) * 2 + side

    def pass_on(i):
        e, place = i // 2, chunk_at(i)
        rows = pl.ds(place * chunk, chunk)
        halves[i].wait_recv()
        both = (num[rows, :, mine] + num_got[rows]).reshape(flat, CYCLES)
        if padded > flat:
            both = jnp.concatenate([both, jnp.zeros((padded - flat, CYCLES), F32)], axis=0)
        if i % 2:
            crossing[e].wait_recv()
            both = both + part_got[e].astype(F32)
            if e == outer - 1:
                own[...] = both
                return
            slot, peer = outer + e, place * 2 + core
        else:
            slot, peer = e, partner
        part_out[slot] = both.astype(BF16)
        copy = remote(
            part_out.at[slot], part_got.at[slot], p_send.at[slot], p_recv.at[slot], wide=peer
        )
        copy.start()
        if i % 2:
            parts.append(copy)
        else:
            crossing.append(copy)

    for i in range(chips):
        place = chunk_at(i)
        coeff = coeffs[place]
        for row in range(chunk):
            lines = pl.ds(pl.multiple_of((place * chunk + row) * pitch, 8), particles)
            x_real, x_imag = spec_re[lines, :], spec_im[lines, :]
            h_real = coeff[:, row : row + 1]
            h_imag = coeff[:, 64 + row : 65 + row]
            a_real = x_real * h_real - x_imag * h_imag
            a_imag = x_real * h_imag + x_imag * h_real
            aligned = jnp.concatenate([a_real, a_imag], axis=-1).astype(BF16)
            sums = jnp.dot(picked, aligned, preferred_element_type=F32)
            num[place * chunk + row] = sums[:CLS_GRP]
        rows = pl.ds(place * chunk, chunk)
        copy = remote(
            num.at[rows, :, theirs], num_got.at[rows], n_send.at[i], n_recv.at[i], wide=sibling
        )
        copy.start()
        halves.append(copy)
        if i % 2:
            pass_on(i - 1)
            if i > 2:
                pass_on(i - 2)
    pass_on(chips - 1)

    peak, total = top[0:1], top[1:2]
    for d in range(1, narrow):
        tops[d - 1].wait_recv()
        other = top_got[d, 0:1]
        joined = jnp.maximum(peak, other)
        total = total * jnp.exp(peak - joined) + top_got[d, 1:2] * jnp.exp(other - joined)
        peak = joined
    ev_ref[...] = peak + jnp.log(total)
    for copy in dens:
        copy.wait_recv()
    scale = den_all[0]
    for e in range(1, chips):
        scale = scale + den_all[e]
    scale = 1.0 / (scale + TAU)
    for copy in parts:
        copy.wait_recv()
    summed = own[...]
    for e in range(outer - 1):
        summed = summed + part_got[outer + e].astype(F32)
    summed = summed[:flat].reshape(chunk, CLS_GRP, CYCLES) * scale[None]
    quads = -(-chunk // OWN_MAX)
    blank = jnp.zeros((CLS_GRP, CYCLES), F32)
    for quad in range(quads):
        four = range(quad * OWN_MAX, (quad + 1) * OWN_MAX)
        four = jnp.concatenate([summed[r] if r < chunk else blank for r in four], axis=0)
        out = jnp.dot(pick[...], four.astype(BF16), preferred_element_type=F32)
        slot_out[:, quad] = out.astype(BF16).reshape(wide, TILE, CYCLES)
    slots = []
    for d in range(1, wide):
        peer = lax.rem(me + d, wide)
        copy = remote(slot_out.at[peer], har.at[core, chip], s_send.at[d], s_recv.at[d], wide=peer)
        copy.start()
        slots.append(copy)
    har[core, chip] = slot_out[me]
    for copy in slots:
        copy.wait_recv()
    length = chips * quads * TILE
    both = jnp.concatenate(
        [har[0].reshape(length, CYCLES), har[1].reshape(length, CYCLES)], axis=1
    )
    out = jnp.dot(back_ref[...], jnp.concatenate([both, both]), preferred_element_type=F32)
    size = OWN_MAX * ANGLES
    by_cos, by_sin = out[:size], out[size:]
    real = by_cos[:, :CYCLES] - by_sin[:, CYCLES:]
    imag = by_cos[:, CYCLES:] + by_sin[:, :CYCLES]
    for slot in range(OWN_MAX):
        span = slice(slot * ANGLES, (slot + 1) * ANGLES)
        new_ref[0, 0, slot, :, :CYCLES] = real[span].astype(BF16)
        new_ref[0, 0, slot, :, CYCLES:] = imag[span].astype(BF16)
    for copy in [den_copy] + first + second + third + fourth + halves + tops + dens + crossing + parts + slots:
        copy.wait_send()


def per_device(images, defocus, class_index, rotation_index, owner_map, roster, ref_store):
    wide = lax.axis_size("wide")
    narrow = lax.axis_size("narrow")
    chips = wide // 2
    chunk = -(-ANGLES // chips)
    quads = -(-chunk // OWN_MAX)
    particles = images.shape[0]
    cosines, sines = tables()

    block_classes = ref_store.shape[2]
    pieces_each = max(wide // (2 * block_classes), 1)
    rows = ANGLES // pieces_each
    height = up(rows, 16)

    dft = np.block([[cosines, sines], [-sines, cosines]]).astype(BF16)
    spaced = np.zeros((2 * ANGLES, 2, pieces_each, height), np.float32)
    spaced[..., :rows] = dft.astype(np.float32).reshape(2 * ANGLES, 2, pieces_each, rows)
    rdft = spaced.reshape(2 * ANGLES, -1).astype(BF16)
    turn = np.concatenate([cosines, -sines], axis=1)
    tab = np.zeros((chips, ANGLES, CYCLES), np.float32)
    back = np.zeros((2, OWN_MAX, ANGLES, chips, quads, OWN_MAX, OWN_MAX), np.float32)
    for m in range(ANGLES):
        place, row = divmod(m, chunk)
        tab[place, :, row] = cosines[:, m]
        tab[place, :, 64 + row] = sines[:, m]
        for slot in range(OWN_MAX):
            back[0, slot, :, place, row // OWN_MAX, row % OWN_MAX, slot] = cosines[m] / ANGLES
            back[1, slot, :, place, row // OWN_MAX, row % OWN_MAX, slot] = sines[m] / ANGLES
    back = back.reshape(2 * OWN_MAX * ANGLES, chips * quads * TILE)
    high, low = high_low(back)
    back = np.concatenate([high, low], axis=1).astype(BF16)
    high, low = high_low(turn)
    turn = np.concatenate([high, high, low], axis=1).astype(BF16)
    high, low = high_low(tab)
    tab = np.concatenate([high, low, high], axis=1).transpose(1, 0, 2).reshape(3 * ANGLES, -1)
    tab = tab.astype(BF16)

    vmem = pl.BlockSpec(memory_space=pltpu.VMEM)
    dma = pltpu.SemaphoreType.DMA
    flat = up(chunk * CLS_GRP, 16)
    new, evidence = pl.pallas_call(
        functools.partial(kernel, wide, narrow, chunk, pieces_each),
        out_shape=(
            jax.ShapeDtypeStruct((1, 1, OWN_MAX, ANGLES, 2 * CYCLES), BF16),
            jax.ShapeDtypeStruct((1, particles), F32),
        ),
        in_specs=[
            pl.BlockSpec(memory_space=pltpu.SMEM), vmem, pl.BlockSpec(memory_space=pl.ANY)
        ] + [vmem] * 9,
        out_specs=(vmem, vmem),
        scratch_shapes=[
            pltpu.VMEM((wide, height, CYCLES), BF16),
            pltpu.VMEM((particles, CYCLES), F32),
            pltpu.VMEM((particles, ANGLES, 2 * CYCLES), BF16),
            pltpu.VMEM((chunk * chips * (particles + 8), CYCLES), F32),
            pltpu.VMEM((chunk * chips * (particles + 8), CYCLES), F32),
            pltpu.VMEM((chips, particles, CYCLES), F32),
            pltpu.VMEM((wide, height, CYCLES), BF16),
            pltpu.VMEM((wide, STEPS, height, CYCLES), BF16),
            pltpu.VMEM((ANGLES * (2 * CLS_GRP + 8), CYCLES), F32),
            pltpu.VMEM((ANGLES * (2 * CLS_GRP + 8), CYCLES), F32),
            pltpu.VMEM((ANGLES * (2 * CLS_GRP + 8), particles), F32),
            pltpu.VMEM((CLS_GRP, ANGLES, particles), F32),
            pltpu.VMEM((chunk * chips, CLS_GRP, 2 * CYCLES), F32),
            pltpu.VMEM((chunk * chips, CLS_GRP, CYCLES), F32),
            pltpu.VMEM((CLS_GRP, CYCLES), F32),
            pltpu.VMEM((CLS_GRP, CYCLES), F32),
            pltpu.VMEM((chips, CLS_GRP, CYCLES), F32),
            pltpu.VMEM((8, particles), F32),
            pltpu.VMEM((narrow, 8, particles), F32),
            pltpu.VMEM((chips, flat, CYCLES), BF16),
            pltpu.VMEM((chips, flat, CYCLES), BF16),
            pltpu.VMEM((flat, CYCLES), F32),
            pltpu.VMEM((wide * TILE, OWN_MAX * CLS_GRP), BF16),
            pltpu.VMEM((wide, quads, TILE, CYCLES), BF16),
            pltpu.VMEM((2, chips, quads, TILE, CYCLES), BF16),
            dma((1,)),
            dma((wide,)), dma((wide,)),
            dma((chips,)), dma((chips,)),
            dma((chips,)), dma((chips,)),
            dma((chips,)), dma((chips,)),
            dma((narrow,)), dma((narrow,)),
            dma((1,)), dma((1,)),
            dma((chips,)), dma((chips,)),
            dma((chips,)), dma((chips,)),
            dma((chips,)), dma((chips,)),
            dma((wide,)), dma((wide,)),
        ],
        compiler_params=pltpu.CompilerParams(
            collective_id=0, has_side_effects=True, vmem_limit_bytes=VMEM_LIMIT
        ),
        name="class_averages",
    )(
        roster, ref_store, images, defocus.reshape(1, particles),
        class_index.reshape(1, particles), rotation_index.reshape(1, particles),
        owner_map.reshape(1, narrow * CLS_GRP),
        jnp.asarray(dft), jnp.asarray(rdft), jnp.asarray(turn), jnp.asarray(tab), jnp.asarray(back),
    )
    return new, evidence.reshape(particles)


def solution(mesh):
    in_specs = (
        P("wide", None, None),
        P("wide"),
        P("wide"),
        P("wide"),
        P(),
        P(),
        P("wide", "narrow", None, None, None),
    )
    out_specs = (P("wide", "narrow", None, None, None), P("wide"))
    return jax.shard_map(
        per_device, mesh=mesh, in_specs=in_specs, out_specs=out_specs, check_vma=False
    )
```
